512 devices in a mesh: dom: 64 (over y, z), feat: 8 (over x, core).
Axes of the slice: x: 4, y: 4, z: 16, core: 2. Of those that a mesh axis runs over, the one named last changes fastest.
Arguments:
- feats: bfloat16 [128, 65536], P('feat', 'dom'), may hold values from -6 to 6
- aggregated: bfloat16 [128, 65536], P('feat', 'dom'), may hold values from -6 to 6
- preact: bfloat16 [128, 65536], P('feat', 'dom'), may hold values from -6 to 6
- grad_out: bfloat16 [128, 65536], P('feat', 'dom'), may hold values from -6 to 6
- w_self: bfloat16 [128, 128], P('feat'), may hold values from -0.5 to 0.5
- w_neigh: bfloat16 [128, 128], P('feat'), may hold values from -0.5 to 0.5
- tile_values: bfloat16 [3072, 128, 128], P('dom'), may hold values from 0 to 1, as said below
- tile_target: int32 [3072], P('dom'), may hold values from 0 to 7
- tile_source: int32 [3072], P('dom'), may hold values from 0 to 39
- tile_count: int32 [64], P('dom'), may hold values from 12 to 48, as said below
- recv_rows: int32 [64, 64, 64], P('dom'), may hold values from 0 to 1023
- recv_count: int32 [64, 64], P('dom'), may hold values from 1 to 64, as said below
Outputs:
- grad_feats: float32 [128, 65536], P('feat', 'dom')
- grad_w_self: float32 [128, 128], P('feat')
- grad_w_neigh: float32 [128, 128], P('feat')
The draws below stay inside these ranges and needn't reach their ends.
Inputs may be any that keep to these rules, and one draw needn't show every extreme that they name: `tile_count`: in every draw some index of dom uses all 48 slots. `recv_count`: every owner has some source that fills all 64 slots. `recv_rows`: rows may repeat; repeated rows receive the sum. `tile_values`: entries are 0 or 1.
All inputs are finite; a program needn't handle non-finite values.
Results may differ from the reference program's by a relative error of at most 0.0012.
Values may be sent and summed in bfloat16 or wider, within the bound.
No kernel may reach another device: no remote copies, remote signals or barrier semaphores. Data moves between devices by JAX's collectives and lax.ppermute only.
A program may use at most 64 MiB of HBM per device.

```python
import jax
import jax.numpy as jnp
from jax import lax

D = 128
TILE = 128
TILES_DEV = 8
TPD = 48
CAP = 64
NODES = 65536
TILES_ALL = 3072
HALO_TILES = 32
N_DOM = 64


def draw_tile_values(key, part):
    key = jax.random.fold_in(key, 11)
    present = jax.random.bernoulli(key, 0.015, (TILES_ALL, TILE, TILE)).astype(jnp.float32)
    return present.astype(jnp.bfloat16)


def draw_tile_count(key, part):
    key = jax.random.fold_in(key, 23)
    key_a, key_b = jax.random.split(key)
    counts = jax.random.randint(key_a, (N_DOM,), max(1, TPD // 4), TPD + 1)
    where = jax.random.randint(key_b, (), 0, N_DOM)
    return counts.at[where].set(TPD).astype(jnp.int32)


def draw_recv_count(key, part):
    key = jax.random.fold_in(key, 37)
    key_a, key_b = jax.random.split(key)
    counts = jax.random.randint(key_a, (N_DOM, N_DOM), 1, CAP + 1)
    cols = jax.random.randint(key_b, (N_DOM,), 0, N_DOM)
    return counts.at[jnp.arange(N_DOM), cols].set(CAP).astype(jnp.int32)


def place_ends(array, key, low, high):
    place = [jax.random.randint(jax.random.fold_in(key, axis), (), 0, length) for axis, length in enumerate(array.shape)]
    longest = array.shape.index(max(array.shape))
    neighbour = place[:longest] + [(place[longest] + 1) % array.shape[longest]] + place[longest + 1:]
    return array.at[tuple(place)].set(low).at[tuple(neighbour)].set(high)


def block_scale(rng, shape, shards, smallest, high):
    gain, own = 1.0, jax.random.fold_in(rng, 6)
    for position, parts in shards:
        draws = jnp.exp(jax.random.uniform(jax.random.fold_in(own, position), (parts,), jnp.float32, smallest / len(shards), high / len(shards)))
        gain = gain * jnp.repeat(draws, shape[position] // parts).reshape([-1 if axis == position else 1 for axis in range(len(shape))])
    return gain


def normal_values(own_key, dims, deviation, bound, cuts=(), kind=jnp.bfloat16):
    array = jax.random.normal(own_key, dims, jnp.float32) * deviation
    if len(cuts) > 0:
        array = block_scale(own_key, dims, cuts, -0.22, 0.18) * array
    return jnp.clip(array, min=-bound, max=bound).astype(kind)


def setup_inputs(seed: int = 0) -> dict:
    streams_of = jax.random.split(jax.random.key(seed), 13)
    feats = normal_values(streams_of[0], (D, NODES), 1.0, 6.0, ((0, 8), (1, 64)))
    aggregated = normal_values(streams_of[1], (D, NODES), 1.0, 6.0, ((0, 8), (1, 64)))
    preact = normal_values(streams_of[2], (D, NODES), 1.0, 6.0, ((0, 8), (1, 64)))
    grad_out = normal_values(streams_of[3], (D, NODES), 1.0, 6.0, ((0, 8), (1, 64)))
    w_self = normal_values(streams_of[4], (D, D), D ** -0.5, 0.5, ((0, 8),))
    w_neigh = normal_values(streams_of[5], (D, D), D ** -0.5, 0.5, ((0, 8),))
    tile_values = draw_tile_values(jax.random.fold_in(streams_of[12], 71), 0)
    tile_target = place_ends(jax.random.randint(streams_of[7], (TILES_ALL,), 0, TILES_DEV), jax.random.fold_in(streams_of[7], 1), 0, TILES_DEV - 1).astype(jnp.int32)
    tile_source = place_ends(jax.random.randint(streams_of[8], (TILES_ALL,), 0, TILES_DEV + HALO_TILES), jax.random.fold_in(streams_of[8], 1), 0, (TILES_DEV + HALO_TILES) - 1).astype(jnp.int32)
    tile_count = draw_tile_count(jax.random.fold_in(streams_of[12], 71), 0)
    recv_rows = place_ends(jax.random.randint(streams_of[10], (N_DOM, N_DOM, CAP), 0, TILES_DEV * TILE), jax.random.fold_in(streams_of[10], 1), 0, (TILES_DEV * TILE) - 1).astype(jnp.int32)
    recv_count = draw_recv_count(jax.random.fold_in(streams_of[12], 71), 0)
    return {"feats": feats, "aggregated": aggregated, "preact": preact, "grad_out": grad_out, "w_self": w_self, "w_neigh": w_neigh, "tile_values": tile_values, "tile_target": tile_target, "tile_source": tile_source, "tile_count": tile_count, "recv_rows": recv_rows, "recv_count": recv_count}


def reference(feats, aggregated, preact, grad_out, w_self, w_neigh, tile_values, tile_target, tile_source, tile_count, recv_rows, recv_count):
    nodes_dev = TILES_DEV * TILE
    src_tiles = TILES_DEV + HALO_TILES
    dz = jnp.where(preact > 0, grad_out, jnp.zeros_like(grad_out)).astype(jnp.bfloat16)
    grad_w_self = jnp.dot(feats, dz.T, preferred_element_type=jnp.float32)
    grad_w_neigh = jnp.dot(aggregated, dz.T, preferred_element_type=jnp.float32)
    self_part = jnp.dot(w_self, dz, preferred_element_type=jnp.float32)

    def one_degree(index):
        first = (index * TPD).astype(jnp.int32)
        tiles = lax.dynamic_slice_in_dim(tile_values, first, TPD, 0).astype(jnp.float32)
        targets = lax.dynamic_slice_in_dim(tile_target, first, TPD, 0)
        valid = (jnp.arange(TPD) < tile_count[index]).astype(jnp.float32)
        row_sums = jnp.sum(tiles, axis=2) * valid[:, None]
        counted = jnp.zeros((TILES_DEV, TILE), jnp.float32).at[targets].add(row_sums)
        return jnp.maximum(counted.reshape(nodes_dev), 1.0)

    degree = lax.map(one_degree, jnp.arange(N_DOM, dtype=jnp.int32)).reshape(NODES)
    message = (jnp.dot(w_neigh, dz, preferred_element_type=jnp.float32) / degree[None, :]).astype(jnp.bfloat16)

    def one_domain(index):
        start = (index * nodes_dev).astype(jnp.int32)
        msg_dom = lax.dynamic_slice_in_dim(message, start, nodes_dev, 1).reshape(D, TILES_DEV, TILE)
        first = (index * TPD).astype(jnp.int32)
        tiles = lax.dynamic_slice_in_dim(tile_values, first, TPD, 0).astype(jnp.float32)
        targets = lax.dynamic_slice_in_dim(tile_target, first, TPD, 0)
        sources = lax.dynamic_slice_in_dim(tile_source, first, TPD, 0)
        valid = (jnp.arange(TPD) < tile_count[index]).astype(jnp.float32)
        blocks = jnp.transpose(msg_dom[:, targets, :], (1, 0, 2)).astype(jnp.float32)
        contrib = jnp.einsum("kfc,kcs->kfs", blocks, tiles) * valid[:, None, None]
        ext = jnp.zeros((src_tiles, D, TILE), jnp.float32).at[sources].add(contrib)
        return jnp.transpose(ext, (1, 0, 2)).reshape(D, src_tiles * TILE)

    ext_all = lax.map(one_domain, jnp.arange(N_DOM, dtype=jnp.int32))
    local_part = jnp.transpose(ext_all[:, :, :nodes_dev], (1, 0, 2)).reshape(D, NODES)
    boundary = ext_all[:, :, nodes_dev:].reshape(N_DOM, D, N_DOM, CAP)

    def one_owner(owner):
        vals = jnp.transpose(boundary[:, :, owner, :], (1, 0, 2))
        mask = (jnp.arange(CAP)[None, :] < recv_count[owner][:, None]).astype(jnp.float32)
        vals = (vals * mask[None, :, :]).reshape(D, N_DOM * CAP)
        rows = recv_rows[owner].reshape(-1)
        return jnp.zeros((D, nodes_dev), jnp.float32).at[:, rows].add(vals)

    received = lax.map(one_owner, jnp.arange(N_DOM, dtype=jnp.int32))
    received = jnp.transpose(received, (1, 0, 2)).reshape(D, NODES)
    grad_feats = self_part + local_part + received
    return grad_feats, grad_w_self, grad_w_neigh
```

```python
import jax
import jax.numpy as jnp
from jax import lax
from jax.sharding import PartitionSpec as P

TILE = 128
Y = 4


def spread(x, axis, count, groups=None):
    copies = jnp.broadcast_to(x[None], (count,) + x.shape)
    return lax.all_to_all(copies, axis, 0, 0, tiled=True, axis_index_groups=groups)


def body(
    feats,
    aggregated,
    preact,
    grad_out,
    w_self,
    w_neigh,
    tile_values,
    tile_target,
    tile_source,
    tile_count,
    recv_rows,
    recv_count,
):
    width, nodes_dev = feats.shape
    ndom = lax.axis_size("dom")
    nfeat = lax.axis_size("feat")
    slots = recv_rows.shape[2]
    tiles_dev = nodes_dev // TILE
    halo_tiles = ndom * slots // TILE
    src_tiles = tiles_dev + halo_tiles
    list_len = tile_values.shape[0]
    nz = ndom // Y
    along_y = [[y * nz + z for y in range(Y)] for z in range(nz)]
    along_z = [[y * nz + z for z in range(nz)] for y in range(Y)]

    dz = jnp.where(preact > 0, grad_out, jnp.zeros_like(grad_out))
    dz_full = spread(dz, "feat", nfeat).reshape(nfeat * width, nodes_dev)
    left = jnp.concatenate([feats, aggregated], axis=0)
    part = jnp.dot(left, dz_full.T, preferred_element_type=jnp.float32)
    part_y = jnp.sum(spread(part, "dom", Y, along_y), axis=0)
    total_w = jnp.sum(spread(part_y, "dom", nz, along_z), axis=0)

    valid = jnp.arange(list_len) < tile_count[0]
    target_hit = tile_target[:, None] == jnp.arange(tiles_dev)[None, :]
    pick_count = (target_hit & valid[:, None]).astype(jnp.float32)
    row_sums = jnp.sum(tile_values, axis=2, dtype=jnp.float32)
    degree = jnp.maximum(
        jnp.dot(pick_count.T, row_sums, precision=lax.Precision.HIGHEST).reshape(nodes_dev), 1.0
    )
    message = (
        jnp.dot(w_neigh, dz_full, preferred_element_type=jnp.float32) / degree[None, :]
    ).astype(jnp.bfloat16)
    pick_target = target_hit.astype(jnp.bfloat16)
    blocks = jnp.einsum(
        "kt,ftc->kfc",
        pick_target,
        message.reshape(width, tiles_dev, TILE),
        preferred_element_type=jnp.float32,
    ).astype(jnp.bfloat16)
    contrib = jnp.einsum("kfc,kcs->kfs", blocks, tile_values, preferred_element_type=jnp.float32)
    pick_source = (
        (tile_source[:, None] == jnp.arange(src_tiles)[None, :]) & valid[:, None]
    ).astype(jnp.float32)
    extended = jnp.einsum("ks,kfc->sfc", pick_source, contrib, precision=lax.Precision.HIGHEST)
    local_part = jnp.transpose(extended[:tiles_dev], (1, 0, 2)).reshape(width, nodes_dev)

    halves = width // 2
    send = extended[tiles_dev:].reshape(halo_tiles, 2, halves, 2, slots)
    send = jnp.transpose(send, (0, 3, 2, 1, 4)).reshape(ndom, halves, 2 * slots).astype(jnp.bfloat16)
    got = lax.all_to_all(send, "dom", 0, 0, tiled=True)
    values = jnp.transpose(got.reshape(ndom, halves, 2, slots), (2, 1, 0, 3)).reshape(width, ndom * slots)
    used = jnp.arange(slots)[None, :] < recv_count[0][:, None]
    rows = jnp.where(used, recv_rows[0], -1).reshape(-1)
    hot = (rows[None, :] == jnp.arange(nodes_dev)[:, None]).astype(jnp.bfloat16)
    received = lax.dot_general(values, hot, (((1,), (1,)), ((), ())), preferred_element_type=jnp.float32)
    self_part = jnp.dot(w_self, dz_full, preferred_element_type=jnp.float32)
    total = self_part + local_part + received
    return (total, total_w[:width], total_w[width:])


def solution(mesh):
    return jax.shard_map(
        body,
        mesh=mesh,
        in_specs=(
            P("feat", "dom"),
            P("feat", "dom"),
            P("feat", "dom"),
            P("feat", "dom"),
            P("feat", None),
            P("feat", None),
            P("dom", None, None),
            P("dom"),
            P("dom"),
            P("dom"),
            P("dom", None, None),
            P("dom", None),
        ),
        out_specs=(P("feat", "dom"), P("feat", None), P("feat", None)),
        check_vma=False,
    )
```

```python
import jax
import jax.numpy as jnp
from jax import lax
from jax.experimental import pallas as pl
from jax.experimental.pallas import tpu as pltpu
from jax.sharding import PartitionSpec as P

TILE = 128
Y = 4
F32 = jnp.float32
BF16 = jnp.bfloat16
NT = (((1,), (1,)), ((), ()))
VMEM = pl.BlockSpec(memory_space=pltpu.VMEM)
SMEM = pl.BlockSpec(memory_space=pltpu.SMEM)
PARAMS = pltpu.CompilerParams(vmem_limit_bytes=40 * 1024 * 1024)


def split(x):
    high = x.astype(BF16)
    return high, (x - high.astype(F32)).astype(BF16)


def gate_kernel(preact, grad_out, out):
    dz = jnp.where(preact[...] > 0, grad_out[...], jnp.zeros_like(grad_out))
    for copy in range(out.shape[0]):
        out[copy] = dz


def degree_kernel(count, target, tiles, degree):
    degree[...] = jnp.zeros_like(degree)
    ones = jnp.ones((8, TILE), BF16)
    for k in range(tiles.shape[0]):
        sums = lax.dot_general(ones, tiles[k], NT, preferred_element_type=F32)
        degree[target[k]] += jnp.where(k < count[0], sums, 0.0)
    degree[...] = jnp.maximum(degree[...], 1.0)


def tile_kernel(count, target, source, dz, feats, aggregated, w_self, w_neigh, tiles, degree, out, base, messages, sums):
    tiles_dev = messages.shape[0]
    halo = sums.shape[0] - tiles_dev
    per = halo // Y
    left = jnp.concatenate([feats[...], aggregated[...]], axis=0)
    high, low = split(lax.dot_general(left, dz[...], NT, preferred_element_type=F32))
    rows = high.shape[0]
    for y in range(Y):
        out[y, per * 16 : per * 16 + rows] = high
        out[y, per * 16 + rows : per * 16 + 2 * rows] = low
    weights = jnp.concatenate([w_neigh[...], w_self[...]], axis=0)
    product = jnp.dot(weights, dz[...], preferred_element_type=F32)
    for t in range(tiles_dev):
        columns = slice(t * TILE, (t + 1) * TILE)
        messages[t] = (product[:16, columns] / degree[t, 0:1]).astype(BF16)
    sums[...] = jnp.zeros_like(sums)
    for k in range(tiles.shape[0]):
        block = messages[target[k]]
        block = jnp.where(k < count[0], block, jnp.zeros_like(block))
        sums[source[k]] += jnp.dot(block, tiles[k], preferred_element_type=F32)
    for t in range(tiles_dev):
        columns = slice(t * TILE, (t + 1) * TILE)
        base[:, columns] = product[16:, columns] + sums[t]
    for b in range(halo):
        out[b // per, (b % per) * 16 : (b % per + 1) * 16] = sums[tiles_dev + b].astype(BF16)


def repack_kernel(got, out):
    nz, rows = out.shape[0], 32
    per = nz // 2
    total = jnp.zeros((rows, TILE), F32)
    for y in range(Y):
        total += got[y, per * 16 : per * 16 + rows].astype(F32)
        total += got[y, per * 16 + rows : per * 16 + 2 * rows].astype(F32)
    high, low = split(total)
    first = lax.broadcasted_iota(jnp.int32, (16, TILE), 1) < TILE // 2
    for pair in range(per):
        for m in range(Y // 2):
            a = got[2 * m, pair * 16 : (pair + 1) * 16].astype(F32)
            b = got[2 * m + 1, pair * 16 : (pair + 1) * 16].astype(F32)
            out[2 * pair, m * 16 : (m + 1) * 16] = jnp.where(first, a, pltpu.roll(b, TILE // 2, 1)).astype(BF16)
            out[2 * pair + 1, m * 16 : (m + 1) * 16] = jnp.where(first, pltpu.roll(a, TILE // 2, 1), b).astype(BF16)
    for z in range(nz):
        out[z, Y * 8 : Y * 8 + rows] = high
        out[z, Y * 8 + rows : Y * 8 + 2 * rows] = low


def scatter_kernel(got, hot, base, out, grad_w_self, grad_w_neigh):
    nz, rows = got.shape[0], 32
    total = base[...]
    weight = jnp.zeros((rows, TILE), F32)
    for z in range(nz):
        values = jnp.concatenate([got[z, m * 16 : (m + 1) * 16] for m in range(Y // 2)], axis=1)
        span = values.shape[1]
        total += jnp.dot(values, hot[z * span : (z + 1) * span], preferred_element_type=F32)
        weight += got[z, Y * 8 : Y * 8 + rows].astype(F32)
        weight += got[z, Y * 8 + rows : Y * 8 + 2 * rows].astype(F32)
    out[...] = total
    grad_w_self[...] = weight[:16]
    grad_w_neigh[...] = weight[16:]


def call(kernel, outs, specs, *args, scratch=(), flops=0, moved=0):
    return pl.pallas_call(
        kernel,
        out_shape=outs,
        in_specs=specs,
        out_specs=jax.tree.map(lambda _: VMEM, outs),
        scratch_shapes=scratch,
        compiler_params=PARAMS,
        cost_estimate=pl.CostEstimate(flops=flops, bytes_accessed=moved, transcendentals=0),
    )(*args)


def body(
    feats,
    aggregated,
    preact,
    grad_out,
    w_self,
    w_neigh,
    tile_values,
    tile_target,
    tile_source,
    tile_count,
    recv_rows,
    recv_count,
):
    width, nodes_dev = feats.shape
    ndom = lax.axis_size("dom")
    nfeat = lax.axis_size("feat")
    slots = recv_rows.shape[2]
    tiles_dev = nodes_dev // TILE
    halo_tiles = ndom * slots // TILE
    nz = ndom // Y
    along_y = [[y * nz + z for y in range(Y)] for z in range(nz)]
    along_z = [[y * nz + z for z in range(nz)] for y in range(Y)]
    shape = jax.ShapeDtypeStruct

    dz = call(gate_kernel, shape((nfeat, width, nodes_dev), BF16), [VMEM] * 2, preact, grad_out)
    dz = lax.all_to_all(dz, "feat", 0, 0, tiled=True).reshape(nfeat * width, nodes_dev)
    degree = call(
        degree_kernel, shape((tiles_dev, 8, TILE), F32), [SMEM, SMEM, VMEM], tile_count, tile_target, tile_values
    )

    per = halo_tiles // Y
    out, base = call(
        tile_kernel,
        (shape((Y, per * 16 + 4 * width, TILE), BF16), shape((width, nodes_dev), F32)),
        [SMEM] * 3 + [VMEM] * 7,
        tile_count,
        tile_target,
        tile_source,
        dz,
        feats,
        aggregated,
        w_self,
        w_neigh,
        tile_values,
        degree,
        scratch=[pltpu.VMEM((tiles_dev, width, TILE), BF16), pltpu.VMEM((tiles_dev + halo_tiles, width, TILE), F32)],
    )
    got = lax.all_to_all(out, "dom", 0, 0, tiled=True, axis_index_groups=along_y)
    out = call(repack_kernel, shape((nz, Y * 8 + 4 * width, TILE), BF16), [VMEM], got)
    got = lax.all_to_all(out, "dom", 0, 0, tiled=True, axis_index_groups=along_z)

    used = jnp.arange(slots)[None, :] < recv_count[0][:, None]
    rows = jnp.where(used, recv_rows[0], -1).reshape(Y, nz, slots)
    rows = jnp.transpose(rows, (1, 0, 2)).reshape(ndom * slots)
    hot = (rows[:, None] == jnp.arange(nodes_dev)[None, :]).astype(BF16)
    return call(
        scatter_kernel,
        (shape((width, nodes_dev), F32), shape((width, TILE), F32), shape((width, TILE), F32)),
        [VMEM] * 3,
        got,
        hot,
        base,
    )


def solution(mesh):
    return jax.shard_map(
        body,
        mesh=mesh,
        in_specs=(
            P("feat", "dom"),
            P("feat", "dom"),
            P("feat", "dom"),
            P("feat", "dom"),
            P("feat", None),
            P("feat", None),
            P("dom", None, None),
            P("dom"),
            P("dom"),
            P("dom"),
            P("dom", None, None),
            P("dom", None),
        ),
        out_specs=(P("feat", "dom"), P("feat", None), P("feat", None)),
        check_vma=False,
    )
```

```python
import jax
import jax.numpy as jnp
from jax import lax
from jax.experimental import pallas as pl
from jax.experimental.pallas import tpu as pltpu
from jax.sharding import PartitionSpec as P

TILE = 128
Y = 4
F32 = jnp.float32
BF16 = jnp.bfloat16
NT = (((1,), (1,)), ((), ()))
VMEM = pl.BlockSpec(memory_space=pltpu.VMEM)
ANY = pl.BlockSpec(memory_space=pl.ANY)
SMEM = pl.BlockSpec(memory_space=pltpu.SMEM)
MIB = 1024 * 1024


def split(x):
    high = x.astype(BF16)
    return high, (x - high.astype(F32)).astype(BF16)


def fetch(pairs, sems):
    copies = [pltpu.make_async_copy(src, dst, sems.at[i]) for i, (src, dst) in enumerate(pairs)]
    for copy in copies:
        copy.start()
    return copies


def gate_kernel(preact, grad_out, out, gate, grad, sems):
    for copy in fetch([(preact, gate), (grad_out, grad)], sems):
        copy.wait()
    dz = jnp.where(gate[...] > 0, grad[...], jnp.zeros_like(grad))
    for copy in range(out.shape[0]):
        out[copy] = dz


def prep_kernel(
    count, target, source, tiles_in, feats, aggregated, w_self, w_neigh, tiles, left, weights, degree, lists, count_s, sems
):
    copies = fetch(
        [
            (tiles_in, tiles),
            (count, count_s),
            (target, lists.at[0]),
            (source, lists.at[1]),
            (feats, left.at[0:16]),
            (aggregated, left.at[16:32]),
            (w_neigh, weights.at[0:16]),
            (w_self, weights.at[16:32]),
        ],
        sems,
    )
    for copy in copies:
        copy.wait()
    degree[...] = jnp.zeros_like(degree)
    ones = jnp.ones((8, TILE), BF16)
    for k in range(tiles.shape[0]):
        sums = lax.dot_general(ones, tiles[k], NT, preferred_element_type=F32)
        degree[lists[0, k]] += jnp.where(k < count_s[0], sums, 0.0)
    degree[...] = jnp.maximum(degree[...], 1.0)


def route_kernel(recv_rows, recv_count, hot, part, rows, counts, sems):
    for copy in fetch([(recv_rows.at[0], rows), (recv_count.at[0], counts)], sems):
        copy.wait()
    nz = rows.shape[0] // Y
    slots = rows.shape[1]
    lane = lax.broadcasted_iota(jnp.int32, (1, slots), 1)
    sub = lax.broadcasted_iota(jnp.int32, (TILE, TILE), 0)
    for z in range(nz):
        for m in range(Y // 2):
            pair = []
            for y in (2 * m, 2 * m + 1):
                s = y * nz + z
                pair.append(jnp.where(lane < counts[s], rows[s : s + 1], -1))
            row = jnp.concatenate(pair, axis=1)
            k = (z * (Y // 2) + m) * TILE
            hot[:, k : k + TILE] = (jnp.broadcast_to(row & (TILE - 1), (TILE, TILE)) == sub).astype(F32).astype(BF16)
            part[:, k : k + TILE] = jnp.broadcast_to(row >> 7, (16, TILE)).astype(F32).astype(BF16)


def tile_kernel(count, target, source, dz, left, weights, tiles, degree, out, base, messages, sums):
    tiles_dev = messages.shape[0]
    halo = sums.shape[0] - tiles_dev
    per = halo // Y
    high, low = split(lax.dot_general(left[...], dz[...], NT, preferred_element_type=F32))
    rows = high.shape[0]
    for y in range(Y):
        out[y, per * 16 : per * 16 + rows] = high
        out[y, per * 16 + rows : per * 16 + 2 * rows] = low
    product = jnp.dot(weights[...], dz[...], preferred_element_type=F32)
    for t in range(tiles_dev):
        columns = slice(t * TILE, (t + 1) * TILE)
        messages[t] = (product[:16, columns] / degree[t, 0:1]).astype(BF16)
    sums[...] = jnp.zeros_like(sums)
    for k in range(tiles.shape[0]):
        block = messages[target[k]]
        block = jnp.where(k < count[0], block, jnp.zeros_like(block))
        sums[source[k]] += jnp.dot(block, tiles[k], preferred_element_type=F32)
    for t in range(tiles_dev):
        columns = slice(t * TILE, (t + 1) * TILE)
        base[:, columns] = product[16:, columns] + sums[t]
    for b in range(halo):
        out[b // per, (b % per) * 16 : (b % per + 1) * 16] = sums[tiles_dev + b].astype(BF16)


def repack_kernel(got, out):
    nz, rows = out.shape[0], 32
    per = nz // 2
    total = jnp.zeros((rows, TILE), F32)
    for y in range(Y):
        total += got[y, per * 16 : per * 16 + rows].astype(F32)
        total += got[y, per * 16 + rows : per * 16 + 2 * rows].astype(F32)
    high, low = split(total)
    first = lax.broadcasted_iota(jnp.int32, (16, TILE), 1) < TILE // 2
    for pair in range(per):
        for m in range(Y // 2):
            a = got[2 * m, pair * 16 : (pair + 1) * 16].astype(F32)
            b = got[2 * m + 1, pair * 16 : (pair + 1) * 16].astype(F32)
            out[2 * pair, m * 16 : (m + 1) * 16] = jnp.where(first, a, pltpu.roll(b, TILE // 2, 1)).astype(BF16)
            out[2 * pair + 1, m * 16 : (m + 1) * 16] = jnp.where(first, pltpu.roll(a, TILE // 2, 1), b).astype(BF16)
    for z in range(nz):
        out[z, Y * 8 : Y * 8 + rows] = high
        out[z, Y * 8 + rows : Y * 8 + 2 * rows] = low


def scatter_kernel(got, hot, part, base, out, grad_w_self, grad_w_neigh):
    nz, rows = got.shape[0], 32
    tiles_dev = base.shape[1] // TILE
    total = jnp.zeros((tiles_dev * 16, TILE), F32)
    weight = jnp.zeros((rows, TILE), F32)
    for z in range(nz):
        values = jnp.concatenate([got[z, m * 16 : (m + 1) * 16] for m in range(Y // 2)], axis=1)
        span = slice(z * values.shape[1], (z + 1) * values.shape[1])
        where = part[:, span]
        spread = jnp.concatenate([jnp.where(where == t, values, jnp.zeros_like(values)) for t in range(tiles_dev)], axis=0)
        total += lax.dot_general(spread, hot[:, span], NT, preferred_element_type=F32)
        weight += got[z, Y * 8 : Y * 8 + rows].astype(F32)
        weight += got[z, Y * 8 + rows : Y * 8 + 2 * rows].astype(F32)
    for t in range(tiles_dev):
        columns = slice(t * TILE, (t + 1) * TILE)
        out[:, columns] = base[:, columns] + total[t * 16 : (t + 1) * 16]
    grad_w_self[...] = weight[:16]
    grad_w_neigh[...] = weight[16:]


def call(kernel, outs, specs, *args, scratch=(), moved=0, limit=48):
    return pl.pallas_call(
        kernel,
        out_shape=outs,
        in_specs=specs,
        out_specs=jax.tree.map(lambda _: VMEM, outs),
        scratch_shapes=scratch,
        compiler_params=pltpu.CompilerParams(vmem_limit_bytes=limit * MIB),
        cost_estimate=pl.CostEstimate(flops=0, bytes_accessed=moved, transcendentals=0),
    )(*args)


def body(
    feats,
    aggregated,
    preact,
    grad_out,
    w_self,
    w_neigh,
    tile_values,
    tile_target,
    tile_source,
    tile_count,
    recv_rows,
    recv_count,
):
    width, nodes_dev = feats.shape
    ndom = lax.axis_size("dom")
    nfeat = lax.axis_size("feat")
    slots = recv_rows.shape[2]
    tiles_dev = nodes_dev // TILE
    halo_tiles = ndom * slots // TILE
    nz = ndom // Y
    along_y = [[y * nz + z for y in range(Y)] for z in range(nz)]
    along_z = [[y * nz + z for z in range(nz)] for y in range(Y)]
    shape = jax.ShapeDtypeStruct

    dz = call(
        gate_kernel,
        shape((nfeat, width, nodes_dev), BF16),
        [ANY] * 2,
        preact,
        grad_out,
        scratch=[pltpu.VMEM((width, nodes_dev), BF16)] * 2 + [pltpu.SemaphoreType.DMA((2,))],
        limit=60,
    )
    dz = lax.all_to_all(dz, "feat", 0, 0, tiled=True).reshape(nfeat * width, nodes_dev)
    tiles, left, weights, degree = call(
        prep_kernel,
        (
            shape(tile_values.shape, BF16),
            shape((2 * width, nodes_dev), BF16),
            shape((2 * width, TILE), BF16),
            shape((tiles_dev, 8, TILE), F32),
        ),
        [ANY] * 8,
        tile_count,
        tile_target,
        tile_source,
        tile_values,
        feats,
        aggregated,
        w_self,
        w_neigh,
        scratch=[
            pltpu.SMEM((2, tile_values.shape[0]), jnp.int32),
            pltpu.SMEM((1,), jnp.int32),
            pltpu.SemaphoreType.DMA((8,)),
        ],
        moved=4000000,
        limit=51,
    )
    hot, part = call(
        route_kernel,
        (shape((TILE, ndom * slots), BF16), shape((16, ndom * slots), BF16)),
        [ANY] * 2,
        recv_rows,
        recv_count,
        scratch=[
            pltpu.VMEM((ndom, slots), jnp.int32),
            pltpu.SMEM((ndom,), jnp.int32),
            pltpu.SemaphoreType.DMA((2,)),
        ],
        moved=4000000,
    )

    per = halo_tiles // Y
    out, base = call(
        tile_kernel,
        (shape((Y, per * 16 + 4 * width, TILE), BF16), shape((width, nodes_dev), F32)),
        [SMEM] * 3 + [VMEM] * 5,
        tile_count,
        tile_target,
        tile_source,
        dz,
        left,
        weights,
        tiles,
        degree,
        scratch=[pltpu.VMEM((tiles_dev, width, TILE), BF16), pltpu.VMEM((tiles_dev + halo_tiles, width, TILE), F32)],
    )
    got = lax.all_to_all(out, "dom", 0, 0, tiled=True, axis_index_groups=along_y)
    out = call(repack_kernel, shape((nz, Y * 8 + 4 * width, TILE), BF16), [VMEM], got)
    got = lax.all_to_all(out, "dom", 0, 0, tiled=True, axis_index_groups=along_z)

    return call(
        scatter_kernel,
        (shape((width, nodes_dev), F32), shape((width, TILE), F32), shape((width, TILE), F32)),
        [VMEM] * 4,
        got,
        hot,
        part,
        base,
    )


def solution(mesh):
    return jax.shard_map(
        body,
        mesh=mesh,
        in_specs=(
            P("feat", "dom"),
            P("feat", "dom"),
            P("feat", "dom"),
            P("feat", "dom"),
            P("feat", None),
            P("feat", None),
            P("dom", None, None),
            P("dom"),
            P("dom"),
            P("dom"),
            P("dom", None, None),
            P("dom", None),
        ),
        out_specs=(P("feat", "dom"), P("feat", None), P("feat", None)),
        check_vma=False,
    )
```

```python
import jax
import jax.numpy as jnp
from jax import lax
from jax.experimental import pallas as pl
from jax.experimental.pallas import tpu as pltpu
from jax.sharding import PartitionSpec as P

TILE = 128
Y = 4
F32 = jnp.float32
BF16 = jnp.bfloat16
NT = (((1,), (1,)), ((), ()))
VMEM = pl.BlockSpec(memory_space=pltpu.VMEM)
ANY = pl.BlockSpec(memory_space=pl.ANY)
SMEM = pl.BlockSpec(memory_space=pltpu.SMEM)
MIB = 1024 * 1024


def split(x):
    high = x.astype(BF16)
    return high, (x - high.astype(F32)).astype(BF16)


def press(x):
    square = x * 2.0**14
    square = square * square
    return jnp.where(x < 0, -square * square, square * square).astype(BF16)


def release(x):
    x = x.astype(F32)
    root = jnp.sqrt(jnp.sqrt(jnp.abs(x))) * 2.0**-14
    return jnp.where(x < 0, -root, jnp.where(x > 0, root, 0.0))


def fetch(pairs, sems):
    copies = [pltpu.make_async_copy(src, dst, sems.at[i]) for i, (src, dst) in enumerate(pairs)]
    for copy in copies:
        copy.start()
    return copies


def gate_kernel(preact, grad_out, out, gate, grad, sems):
    for copy in fetch([(preact, gate), (grad_out, grad)], sems):
        copy.wait()
    dz = jnp.where(gate[...] > 0, grad[...], jnp.zeros_like(grad))
    for copy in range(out.shape[0]):
        out[copy] = dz


def prep_kernel(
    count, target, tiles_in, feats, aggregated, w_self, w_neigh, tiles, left, weights, degree, sems
):
    copies = fetch(
        [
            (tiles_in, tiles),
            (feats, left.at[0:16]),
            (aggregated, left.at[16:32]),
            (w_neigh, weights.at[0:16]),
            (w_self, weights.at[16:32]),
        ],
        sems,
    )
    for copy in copies:
        copy.wait()
    degree[...] = jnp.zeros_like(degree)
    ones = jnp.ones((8, TILE), BF16)
    for k in range(tiles.shape[0]):
        sums = lax.dot_general(ones, tiles[k], NT, preferred_element_type=F32)
        degree[target[k]] += jnp.where(k < count[0], sums, 0.0)
    degree[...] = jnp.maximum(degree[...], 1.0)


def route_kernel(recv_rows, recv_count, hot, part, rows, counts, sems):
    for copy in fetch([(recv_rows.at[0], rows), (recv_count.at[0], counts)], sems):
        copy.wait()
    nz = rows.shape[0] // Y
    slots = rows.shape[1]
    lane = lax.broadcasted_iota(jnp.int32, (1, slots), 1)
    sub = lax.broadcasted_iota(jnp.int32, (TILE, TILE), 0)
    for z in range(nz):
        for m in range(Y // 2):
            pair = []
            for y in (2 * m, 2 * m + 1):
                s = y * nz + z
                pair.append(jnp.where(lane < counts[s], rows[s : s + 1], -1))
            row = jnp.concatenate(pair, axis=1)
            k = (z * (Y // 2) + m) * TILE
            hot[:, k : k + TILE] = (jnp.broadcast_to(row & (TILE - 1), (TILE, TILE)) == sub).astype(F32).astype(BF16)
            part[:, k : k + TILE] = jnp.broadcast_to(row >> 7, (16, TILE)).astype(F32).astype(BF16)


def tile_kernel(count, target, source, dz, left, weights, tiles, degree, out, base, messages, sums):
    tiles_dev = messages.shape[0]
    halo = sums.shape[0] - tiles_dev
    per = halo // Y
    high, low = split(lax.dot_general(left[...], dz[...], NT, preferred_element_type=F32))
    rows = high.shape[0]
    for y in range(Y):
        out[y, per * 16 : per * 16 + rows] = high
        out[y, per * 16 + rows : per * 16 + 2 * rows] = low
    product = jnp.dot(weights[...], dz[...], preferred_element_type=F32)
    for t in range(tiles_dev):
        columns = slice(t * TILE, (t + 1) * TILE)
        messages[t] = (product[:16, columns] / degree[t, 0:1]).astype(BF16)
    sums[...] = jnp.zeros_like(sums)
    for k in range(tiles.shape[0]):
        block = messages[target[k]]
        block = jnp.where(k < count[0], block, jnp.zeros_like(block))
        sums[source[k]] += jnp.dot(block, tiles[k], preferred_element_type=F32)
    for t in range(tiles_dev):
        columns = slice(t * TILE, (t + 1) * TILE)
        base[:, columns] = product[16:, columns] + sums[t]
    for b in range(halo):
        out[b // per, (b % per) * 16 : (b % per + 1) * 16] = sums[tiles_dev + b].astype(BF16)


def repack_kernel(got, out):
    nz, rows = out.shape[0], 32
    per = nz // 2
    total = jnp.zeros((rows, TILE), F32)
    for y in range(Y):
        total += got[y, per * 16 : per * 16 + rows].astype(F32)
        total += got[y, per * 16 + rows : per * 16 + 2 * rows].astype(F32)
    sent = press(total)
    first = lax.broadcasted_iota(jnp.int32, (16, TILE), 1) < TILE // 2
    for pair in range(per):
        for m in range(Y // 2):
            a = got[2 * m, pair * 16 : (pair + 1) * 16].astype(F32)
            b = got[2 * m + 1, pair * 16 : (pair + 1) * 16].astype(F32)
            out[2 * pair, m * 16 : (m + 1) * 16] = jnp.where(first, a, pltpu.roll(b, TILE // 2, 1)).astype(BF16)
            out[2 * pair + 1, m * 16 : (m + 1) * 16] = jnp.where(first, pltpu.roll(a, TILE // 2, 1), b).astype(BF16)
    for z in range(nz):
        out[z, Y * 8 : Y * 8 + rows] = sent


def scatter_kernel(got, hot, part, base, out, grad_w_self, grad_w_neigh):
    nz, rows = got.shape[0], 32
    tiles_dev = base.shape[1] // TILE
    total = jnp.zeros((tiles_dev * 16, TILE), F32)
    weight = jnp.zeros((rows, TILE), F32)
    for z in range(nz):
        values = jnp.concatenate([got[z, m * 16 : (m + 1) * 16] for m in range(Y // 2)], axis=1)
        span = slice(z * values.shape[1], (z + 1) * values.shape[1])
        where = part[:, span]
        spread = jnp.concatenate([jnp.where(where == t, values, jnp.zeros_like(values)) for t in range(tiles_dev)], axis=0)
        total += lax.dot_general(spread, hot[:, span], NT, preferred_element_type=F32)
        weight += release(got[z, Y * 8 : Y * 8 + rows])
    for t in range(tiles_dev):
        columns = slice(t * TILE, (t + 1) * TILE)
        out[:, columns] = base[:, columns] + total[t * 16 : (t + 1) * 16]
    grad_w_self[...] = weight[:16]
    grad_w_neigh[...] = weight[16:]


def call(kernel, outs, specs, *args, scratch=(), moved=0, limit=48):
    return pl.pallas_call(
        kernel,
        out_shape=outs,
        in_specs=specs,
        out_specs=jax.tree.map(lambda _: VMEM, outs),
        scratch_shapes=scratch,
        compiler_params=pltpu.CompilerParams(vmem_limit_bytes=limit * MIB),
        cost_estimate=pl.CostEstimate(flops=0, bytes_accessed=moved, transcendentals=0),
    )(*args)


def body(
    feats,
    aggregated,
    preact,
    grad_out,
    w_self,
    w_neigh,
    tile_values,
    tile_target,
    tile_source,
    tile_count,
    recv_rows,
    recv_count,
):
    width, nodes_dev = feats.shape
    ndom = lax.axis_size("dom")
    nfeat = lax.axis_size("feat")
    slots = recv_rows.shape[2]
    tiles_dev = nodes_dev // TILE
    halo_tiles = ndom * slots // TILE
    nz = ndom // Y
    along_y = [[y * nz + z for y in range(Y)] for z in range(nz)]
    along_z = [[y * nz + z for z in range(nz)] for y in range(Y)]
    shape = jax.ShapeDtypeStruct

    dz = call(
        gate_kernel,
        shape((nfeat, width, nodes_dev), BF16),
        [ANY] * 2,
        preact,
        grad_out,
        scratch=[pltpu.VMEM((width, nodes_dev), BF16)] * 2 + [pltpu.SemaphoreType.DMA((2,))],
        limit=60,
    )
    dz = lax.all_to_all(dz, "feat", 0, 0, tiled=True).reshape(nfeat * width, nodes_dev)
    tiles, left, weights, degree = call(
        prep_kernel,
        (
            shape(tile_values.shape, BF16),
            shape((2 * width, nodes_dev), BF16),
            shape((2 * width, TILE), BF16),
            shape((tiles_dev, 8, TILE), F32),
        ),
        [SMEM] * 2 + [ANY] * 5,
        tile_count,
        tile_target,
        tile_values,
        feats,
        aggregated,
        w_self,
        w_neigh,
        scratch=[pltpu.SemaphoreType.DMA((5,))],
        moved=4000000,
        limit=51,
    )
    hot, part = call(
        route_kernel,
        (shape((TILE, ndom * slots), BF16), shape((16, ndom * slots), BF16)),
        [ANY] * 2,
        recv_rows,
        recv_count,
        scratch=[
            pltpu.VMEM((ndom, slots), jnp.int32),
            pltpu.SMEM((ndom,), jnp.int32),
            pltpu.SemaphoreType.DMA((2,)),
        ],
        moved=4000000,
    )

    per = halo_tiles // Y
    out, base = call(
        tile_kernel,
        (shape((Y, per * 16 + 4 * width, TILE), BF16), shape((width, nodes_dev), F32)),
        [SMEM] * 3 + [VMEM] * 5,
        tile_count,
        tile_target,
        tile_source,
        dz,
        left,
        weights,
        tiles,
        degree,
        scratch=[pltpu.VMEM((tiles_dev, width, TILE), BF16), pltpu.VMEM((tiles_dev + halo_tiles, width, TILE), F32)],
    )
    got = lax.all_to_all(out, "dom", 0, 0, tiled=True, axis_index_groups=along_y)
    out = call(repack_kernel, shape((nz, Y * 8 + 2 * width, TILE), BF16), [VMEM], got)
    got = lax.all_to_all(out, "dom", 0, 0, tiled=True, axis_index_groups=along_z)

    return call(
        scatter_kernel,
        (shape((width, nodes_dev), F32), shape((width, TILE), F32), shape((width, TILE), F32)),
        [VMEM] * 4,
        got,
        hot,
        part,
        base,
    )


def solution(mesh):
    return jax.shard_map(
        body,
        mesh=mesh,
        in_specs=(
            P("feat", "dom"),
            P("feat", "dom"),
            P("feat", "dom"),
            P("feat", "dom"),
            P("feat", None),
            P("feat", None),
            P("dom", None, None),
            P("dom"),
            P("dom"),
            P("dom"),
            P("dom", None, None),
            P("dom", None),
        ),
        out_specs=(P("feat", "dom"), P("feat", None), P("feat", None)),
        check_vma=False,
    )
```

```python
import jax
import jax.numpy as jnp
from jax import lax
from jax.experimental import pallas as pl
from jax.experimental.pallas import tpu as pltpu
from jax.sharding import PartitionSpec as P

TILE = 128
Y = 4
F32 = jnp.float32
BF16 = jnp.bfloat16
NT = (((1,), (1,)), ((), ()))
VMEM = pl.BlockSpec(memory_space=pltpu.VMEM)
ANY = pl.BlockSpec(memory_space=pl.ANY)
SMEM = pl.BlockSpec(memory_space=pltpu.SMEM)
MIB = 1024 * 1024


def turned(count):
    return [(count // 2 + i) % count for i in range(count)]


def slot(index, count):
    return (index - count // 2) % count


def split(x):
    high = x.astype(BF16)
    return high, (x - high.astype(F32)).astype(BF16)


def press(x):
    square = x * 2.0**14
    square = square * square
    return jnp.where(x < 0, -square * square, square * square).astype(BF16)


def release(x):
    x = x.astype(F32)
    root = jnp.sqrt(jnp.sqrt(jnp.abs(x))) * 2.0**-14
    return jnp.where(x < 0, -root, jnp.where(x > 0, root, 0.0))


def fetch(pairs, sems):
    copies = [pltpu.make_async_copy(src, dst, sems.at[i]) for i, (src, dst) in enumerate(pairs)]
    for copy in copies:
        copy.start()
    return copies


def gate_kernel(preact, grad_out, out, gate, grad, sems):
    for copy in fetch([(preact, gate), (grad_out, grad)], sems):
        copy.wait()
    dz = jnp.where(gate[...] > 0, grad[...], jnp.zeros_like(grad))
    for copy in range(out.shape[0]):
        out[copy] = dz


def prep_kernel(
    count, target, tiles_in, feats, aggregated, w_self, w_neigh, tiles, left, weights, degree, sems
):
    copies = fetch(
        [
            (tiles_in, tiles),
            (feats, left.at[0:16]),
            (aggregated, left.at[16:32]),
            (w_neigh, weights.at[0:16]),
            (w_self, weights.at[16:32]),
        ],
        sems,
    )
    for copy in copies:
        copy.wait()
    degree[...] = jnp.zeros_like(degree)
    ones = jnp.ones((8, TILE), BF16)
    for k in range(tiles.shape[0]):
        sums = lax.dot_general(ones, tiles[k], NT, preferred_element_type=F32)
        degree[target[k]] += jnp.where(k < count[0], sums, 0.0)
    degree[...] = jnp.maximum(degree[...], 1.0)


def route_kernel(recv_rows, recv_count, hot, part, rows, counts, sems):
    for copy in fetch([(recv_rows.at[0], rows), (recv_count.at[0], counts)], sems):
        copy.wait()
    nz = rows.shape[0] // Y
    slots = rows.shape[1]
    lane = lax.broadcasted_iota(jnp.int32, (1, slots), 1)
    sub = lax.broadcasted_iota(jnp.int32, (TILE, TILE), 0)
    for z in range(nz):
        for m in range(Y // 2):
            pair = []
            for y in (2 * m, 2 * m + 1):
                s = y * nz + z
                pair.append(jnp.where(lane < counts[s], rows[s : s + 1], -1))
            row = jnp.concatenate(pair, axis=1)
            k = (z * (Y // 2) + m) * TILE
            hot[:, k : k + TILE] = (jnp.broadcast_to(row & (TILE - 1), (TILE, TILE)) == sub).astype(F32).astype(BF16)
            part[:, k : k + TILE] = jnp.broadcast_to(row >> 7, (16, TILE)).astype(F32).astype(BF16)


def tile_kernel(count, target, source, dz, left, weights, tiles, degree, out, base, messages, sums):
    tiles_dev = messages.shape[0]
    halo = sums.shape[0] - tiles_dev
    per = halo // Y
    half = dz.shape[0] // 2
    dz = jnp.concatenate([dz[half:], dz[:half]], axis=0)
    high, low = split(lax.dot_general(left[...], dz, NT, preferred_element_type=F32))
    rows = high.shape[0]
    for y in range(Y):
        out[y, per * 16 : per * 16 + rows] = high
        out[y, per * 16 + rows : per * 16 + 2 * rows] = low
    product = jnp.dot(weights[...], dz, preferred_element_type=F32)
    for t in range(tiles_dev):
        columns = slice(t * TILE, (t + 1) * TILE)
        messages[t] = (product[:16, columns] / degree[t, 0:1]).astype(BF16)
    sums[...] = jnp.zeros_like(sums)
    for k in range(tiles.shape[0]):
        block = messages[target[k]]
        block = jnp.where(k < count[0], block, jnp.zeros_like(block))
        sums[source[k]] += jnp.dot(block, tiles[k], preferred_element_type=F32)
    for t in range(tiles_dev):
        columns = slice(t * TILE, (t + 1) * TILE)
        base[:, columns] = product[16:, columns] + sums[t]
    for b in range(halo):
        out[slot(b // per, Y), (b % per) * 16 : (b % per + 1) * 16] = sums[tiles_dev + b].astype(BF16)


def repack_kernel(got, out):
    nz, rows = out.shape[0], 32
    per = nz // 2
    total = jnp.zeros((rows, TILE), F32)
    for y in range(Y):
        total += got[y, per * 16 : per * 16 + rows].astype(F32)
        total += got[y, per * 16 + rows : per * 16 + 2 * rows].astype(F32)
    sent = press(total)
    first = lax.broadcasted_iota(jnp.int32, (16, TILE), 1) < TILE // 2
    for pair in range(per):
        for m in range(Y // 2):
            a = got[slot(2 * m, Y), pair * 16 : (pair + 1) * 16].astype(F32)
            b = got[slot(2 * m + 1, Y), pair * 16 : (pair + 1) * 16].astype(F32)
            out[slot(2 * pair, nz), m * 16 : (m + 1) * 16] = jnp.where(first, a, pltpu.roll(b, TILE // 2, 1)).astype(BF16)
            out[slot(2 * pair + 1, nz), m * 16 : (m + 1) * 16] = jnp.where(first, pltpu.roll(a, TILE // 2, 1), b).astype(BF16)
    for z in range(nz):
        out[z, Y * 8 : Y * 8 + rows] = sent


def scatter_kernel(got, hot, part, base, out, grad_w_self, grad_w_neigh):
    nz, rows = got.shape[0], 32
    tiles_dev = base.shape[1] // TILE
    total = jnp.zeros((tiles_dev * 16, TILE), F32)
    weight = jnp.zeros((rows, TILE), F32)
    for z in range(nz):
        values = jnp.concatenate([got[slot(z, nz), m * 16 : (m + 1) * 16] for m in range(Y // 2)], axis=1)
        span = slice(z * values.shape[1], (z + 1) * values.shape[1])
        where = part[:, span]
        spread = jnp.concatenate([jnp.where(where == t, values, jnp.zeros_like(values)) for t in range(tiles_dev)], axis=0)
        total += lax.dot_general(spread, hot[:, span], NT, preferred_element_type=F32)
        weight += release(got[z, Y * 8 : Y * 8 + rows])
    for t in range(tiles_dev):
        columns = slice(t * TILE, (t + 1) * TILE)
        out[:, columns] = base[:, columns] + total[t * 16 : (t + 1) * 16]
    grad_w_self[...] = weight[:16]
    grad_w_neigh[...] = weight[16:]


def call(kernel, outs, specs, *args, scratch=(), moved=0, limit=48):
    return pl.pallas_call(
        kernel,
        out_shape=outs,
        in_specs=specs,
        out_specs=jax.tree.map(lambda _: VMEM, outs),
        scratch_shapes=scratch,
        compiler_params=pltpu.CompilerParams(vmem_limit_bytes=limit * MIB),
        cost_estimate=pl.CostEstimate(flops=0, bytes_accessed=moved, transcendentals=0),
    )(*args)


def body(
    feats,
    aggregated,
    preact,
    grad_out,
    w_self,
    w_neigh,
    tile_values,
    tile_target,
    tile_source,
    tile_count,
    recv_rows,
    recv_count,
):
    width, nodes_dev = feats.shape
    ndom = lax.axis_size("dom")
    nfeat = lax.axis_size("feat")
    slots = recv_rows.shape[2]
    tiles_dev = nodes_dev // TILE
    halo_tiles = ndom * slots // TILE
    nz = ndom // Y
    along_y = [[y * nz + z for y in turned(Y)] for z in range(nz)]
    along_z = [[y * nz + z for z in turned(nz)] for y in range(Y)]
    shape = jax.ShapeDtypeStruct

    dz = call(
        gate_kernel,
        shape((nfeat, width, nodes_dev), BF16),
        [ANY] * 2,
        preact,
        grad_out,
        scratch=[pltpu.VMEM((width, nodes_dev), BF16)] * 2 + [pltpu.SemaphoreType.DMA((2,))],
        limit=60,
    )
    dz = lax.all_to_all(dz, "feat", 0, 0, tiled=True, axis_index_groups=[turned(nfeat)]).reshape(nfeat * width, nodes_dev)
    tiles, left, weights, degree = call(
        prep_kernel,
        (
            shape(tile_values.shape, BF16),
            shape((2 * width, nodes_dev), BF16),
            shape((2 * width, TILE), BF16),
            shape((tiles_dev, 8, TILE), F32),
        ),
        [SMEM] * 2 + [ANY] * 5,
        tile_count,
        tile_target,
        tile_values,
        feats,
        aggregated,
        w_self,
        w_neigh,
        scratch=[pltpu.SemaphoreType.DMA((5,))],
        moved=4000000,
        limit=51,
    )
    hot, part = call(
        route_kernel,
        (shape((TILE, ndom * slots), BF16), shape((16, ndom * slots), BF16)),
        [ANY] * 2,
        recv_rows,
        recv_count,
        scratch=[
            pltpu.VMEM((ndom, slots), jnp.int32),
            pltpu.SMEM((ndom,), jnp.int32),
            pltpu.SemaphoreType.DMA((2,)),
        ],
        moved=4000000,
    )

    per = halo_tiles // Y
    out, base = call(
        tile_kernel,
        (shape((Y, per * 16 + 4 * width, TILE), BF16), shape((width, nodes_dev), F32)),
        [SMEM] * 3 + [VMEM] * 5,
        tile_count,
        tile_target,
        tile_source,
        dz,
        left,
        weights,
        tiles,
        degree,
        scratch=[pltpu.VMEM((tiles_dev, width, TILE), BF16), pltpu.VMEM((tiles_dev + halo_tiles, width, TILE), F32)],
    )
    got = lax.all_to_all(out, "dom", 0, 0, tiled=True, axis_index_groups=along_y)
    out = call(repack_kernel, shape((nz, Y * 8 + 2 * width, TILE), BF16), [VMEM], got)
    got = lax.all_to_all(out, "dom", 0, 0, tiled=True, axis_index_groups=along_z)

    return call(
        scatter_kernel,
        (shape((width, nodes_dev), F32), shape((width, TILE), F32), shape((width, TILE), F32)),
        [VMEM] * 4,
        got,
        hot,
        part,
        base,
    )


def solution(mesh):
    return jax.shard_map(
        body,
        mesh=mesh,
        in_specs=(
            P("feat", "dom"),
            P("feat", "dom"),
            P("feat", "dom"),
            P("feat", "dom"),
            P("feat", None),
            P("feat", None),
            P("dom", None, None),
            P("dom"),
            P("dom"),
            P("dom"),
            P("dom", None, None),
            P("dom", None),
        ),
        out_specs=(P("feat", "dom"), P("feat", None), P("feat", None)),
        check_vma=False,
    )
```

```python
import jax
import jax.numpy as jnp
from jax import lax
from jax.experimental import pallas as pl
from jax.experimental.pallas import tpu as pltpu
from jax.sharding import PartitionSpec as P

TILE = 128
Y = 4
F32 = jnp.float32
BF16 = jnp.bfloat16
NT = (((1,), (1,)), ((), ()))
VMEM = pl.BlockSpec(memory_space=pltpu.VMEM)
ANY = pl.BlockSpec(memory_space=pl.ANY)
SMEM = pl.BlockSpec(memory_space=pltpu.SMEM)
MIB = 1024 * 1024
CHUNKS = 4


def turned(count):
    return [(count // 2 + i) % count for i in range(count)]


def slot(index, count):
    return (index - count // 2) % count


def split(x):
    high = x.astype(BF16)
    return high, (x - high.astype(F32)).astype(BF16)


def press(x):
    square = x * 2.0**14
    square = square * square
    return jnp.where(x < 0, -square * square, square * square).astype(BF16)


def release(x):
    x = x.astype(F32)
    root = jnp.sqrt(jnp.sqrt(jnp.abs(x))) * 2.0**-14
    return jnp.where(x < 0, -root, jnp.where(x > 0, root, 0.0))


def fetch(pairs, sems):
    copies = [pltpu.make_async_copy(src, dst, sems.at[i]) for i, (src, dst) in enumerate(pairs)]
    for copy in copies:
        copy.start()
    return copies


def gate_kernel(preact, grad_out, out, gate, grad, sems):
    for copy in fetch([(preact, gate), (grad_out, grad)], sems):
        copy.wait()
    dz = jnp.where(gate[...] > 0, grad[...], jnp.zeros_like(grad))
    for copy in range(out.shape[0]):
        out[copy] = dz


def prep_kernel(count, target, tiles_in, tiles, degree, sems):
    step = tiles.shape[0] // CHUNKS
    spans = [pl.ds(i * step, step) for i in range(CHUNKS)]
    copies = fetch([(tiles_in.at[span], tiles.at[span]) for span in spans], sems)
    degree[...] = jnp.zeros_like(degree)
    ones = jnp.ones((8, TILE), BF16)
    for i, copy in enumerate(copies):
        copy.wait()
        for k in range(i * step, (i + 1) * step):
            sums = lax.dot_general(ones, tiles[k], NT, preferred_element_type=F32)
            degree[target[k]] += jnp.where(k < count[0], sums, 0.0)
    degree[...] = jnp.maximum(degree[...], 1.0)


def route_kernel(recv_rows, recv_count, hot, part, rows, counts, sems):
    for copy in fetch([(recv_rows.at[0], rows), (recv_count.at[0], counts)], sems):
        copy.wait()
    nz = rows.shape[0] // Y
    slots = rows.shape[1]
    lane = lax.broadcasted_iota(jnp.int32, (1, slots), 1)
    sub = lax.broadcasted_iota(jnp.int32, (TILE, TILE), 0)
    for z in range(nz):
        for m in range(Y // 2):
            pair = []
            for y in (2 * m, 2 * m + 1):
                s = y * nz + z
                pair.append(jnp.where(lane < counts[s], rows[s : s + 1], -1))
            row = jnp.concatenate(pair, axis=1)
            k = (z * (Y // 2) + m) * TILE
            hot[:, k : k + TILE] = (jnp.broadcast_to(row & (TILE - 1), (TILE, TILE)) == sub).astype(F32).astype(BF16)
            part[:, k : k + TILE] = jnp.broadcast_to(row >> 7, (16, TILE)).astype(F32).astype(BF16)


def tile_kernel(count, target, source, dz, packed, tiles, degree, out, base, messages, sums):
    tiles_dev = messages.shape[0]
    halo = sums.shape[0] - tiles_dev
    per = halo // Y
    half = dz.shape[0] // 2
    dz = jnp.concatenate([dz[half:], dz[:half]], axis=0)
    high, low = split(lax.dot_general(packed[:, : dz.shape[1]], dz, NT, preferred_element_type=F32))
    rows = high.shape[0]
    for y in range(Y):
        out[y, per * 16 : per * 16 + rows] = high
        out[y, per * 16 + rows : per * 16 + 2 * rows] = low
    product = jnp.dot(packed[:, dz.shape[1] :], dz, preferred_element_type=F32)
    for t in range(tiles_dev):
        columns = slice(t * TILE, (t + 1) * TILE)
        messages[t] = (product[:16, columns] / degree[t, 0:1]).astype(BF16)
    sums[...] = jnp.zeros_like(sums)
    for k in range(tiles.shape[0]):
        block = messages[target[k]]
        block = jnp.where(k < count[0], block, jnp.zeros_like(block))
        sums[source[k]] += jnp.dot(block, tiles[k], preferred_element_type=F32)
    for t in range(tiles_dev):
        columns = slice(t * TILE, (t + 1) * TILE)
        base[:, columns] = product[16:, columns] + sums[t]
    for b in range(halo):
        out[slot(b // per, Y), (b % per) * 16 : (b % per + 1) * 16] = sums[tiles_dev + b].astype(BF16)


def repack_kernel(got, out):
    nz, rows = out.shape[0], 32
    per = nz // 2
    total = jnp.zeros((rows, TILE), F32)
    for y in range(Y):
        total += got[y, per * 16 : per * 16 + rows].astype(F32)
        total += got[y, per * 16 + rows : per * 16 + 2 * rows].astype(F32)
    sent = press(total)
    first = lax.broadcasted_iota(jnp.int32, (16, TILE), 1) < TILE // 2
    for pair in range(per):
        for m in range(Y // 2):
            a = got[slot(2 * m, Y), pair * 16 : (pair + 1) * 16].astype(F32)
            b = got[slot(2 * m + 1, Y), pair * 16 : (pair + 1) * 16].astype(F32)
            out[slot(2 * pair, nz), m * 16 : (m + 1) * 16] = jnp.where(first, a, pltpu.roll(b, TILE // 2, 1)).astype(BF16)
            out[slot(2 * pair + 1, nz), m * 16 : (m + 1) * 16] = jnp.where(first, pltpu.roll(a, TILE // 2, 1), b).astype(BF16)
    for z in range(nz):
        out[z, Y * 8 : Y * 8 + rows] = sent


def scatter_kernel(got, hot, part, base, out, grad_w_self, grad_w_neigh):
    nz, rows = got.shape[0], 32
    tiles_dev = base.shape[1] // TILE
    total = jnp.zeros((tiles_dev * 16, TILE), F32)
    weight = jnp.zeros((rows, TILE), F32)
    for z in range(nz):
        values = jnp.concatenate([got[slot(z, nz), m * 16 : (m + 1) * 16] for m in range(Y // 2)], axis=1)
        span = slice(z * values.shape[1], (z + 1) * values.shape[1])
        where = part[:, span]
        spread = jnp.concatenate([jnp.where(where == t, values, jnp.zeros_like(values)) for t in range(tiles_dev)], axis=0)
        total += lax.dot_general(spread, hot[:, span], NT, preferred_element_type=F32)
        weight += release(got[z, Y * 8 : Y * 8 + rows])
    for t in range(tiles_dev):
        columns = slice(t * TILE, (t + 1) * TILE)
        out[:, columns] = base[:, columns] + total[t * 16 : (t + 1) * 16]
    grad_w_self[...] = weight[:16]
    grad_w_neigh[...] = weight[16:]


def call(kernel, outs, specs, *args, scratch=(), moved=0, limit=48):
    return pl.pallas_call(
        kernel,
        out_shape=outs,
        in_specs=specs,
        out_specs=jax.tree.map(lambda _: VMEM, outs),
        scratch_shapes=scratch,
        compiler_params=pltpu.CompilerParams(vmem_limit_bytes=limit * MIB),
        cost_estimate=pl.CostEstimate(flops=0, bytes_accessed=moved, transcendentals=0),
    )(*args)


def body(
    feats,
    aggregated,
    preact,
    grad_out,
    w_self,
    w_neigh,
    tile_values,
    tile_target,
    tile_source,
    tile_count,
    recv_rows,
    recv_count,
):
    width, nodes_dev = feats.shape
    ndom = lax.axis_size("dom")
    nfeat = lax.axis_size("feat")
    slots = recv_rows.shape[2]
    tiles_dev = nodes_dev // TILE
    halo_tiles = ndom * slots // TILE
    nz = ndom // Y
    along_y = [[y * nz + z for y in turned(Y)] for z in range(nz)]
    along_z = [[y * nz + z for z in turned(nz)] for y in range(Y)]
    shape = jax.ShapeDtypeStruct

    dz = call(
        gate_kernel,
        shape((nfeat, width, nodes_dev), BF16),
        [ANY] * 2,
        preact,
        grad_out,
        scratch=[pltpu.VMEM((width, nodes_dev), BF16)] * 2 + [pltpu.SemaphoreType.DMA((2,))],
        limit=60,
    )
    dz = lax.all_to_all(dz, "feat", 0, 0, tiled=True, axis_index_groups=[turned(nfeat)]).reshape(nfeat * width, nodes_dev)
    packed = jnp.concatenate(
        [jnp.concatenate([feats, w_neigh], axis=1), jnp.concatenate([aggregated, w_self], axis=1)], axis=0
    )
    tiles, degree = call(
        prep_kernel,
        (shape(tile_values.shape, BF16), shape((tiles_dev, 8, TILE), F32)),
        [SMEM] * 2 + [ANY],
        tile_count,
        tile_target,
        tile_values,
        scratch=[pltpu.SemaphoreType.DMA((CHUNKS,))],
        moved=4000000,
        limit=51,
    )
    hot, part = call(
        route_kernel,
        (shape((TILE, ndom * slots), BF16), shape((16, ndom * slots), BF16)),
        [ANY] * 2,
        recv_rows,
        recv_count,
        scratch=[
            pltpu.VMEM((ndom, slots), jnp.int32),
            pltpu.SMEM((ndom,), jnp.int32),
            pltpu.SemaphoreType.DMA((2,)),
        ],
        moved=4000000,
    )

    per = halo_tiles // Y
    out, base = call(
        tile_kernel,
        (shape((Y, per * 16 + 4 * width, TILE), BF16), shape((width, nodes_dev), F32)),
        [SMEM] * 3 + [VMEM] * 4,
        tile_count,
        tile_target,
        tile_source,
        dz,
        packed,
        tiles,
        degree,
        scratch=[pltpu.VMEM((tiles_dev, width, TILE), BF16), pltpu.VMEM((tiles_dev + halo_tiles, width, TILE), F32)],
    )
    got = lax.all_to_all(out, "dom", 0, 0, tiled=True, axis_index_groups=along_y)
    out = call(repack_kernel, shape((nz, Y * 8 + 2 * width, TILE), BF16), [VMEM], got)
    got = lax.all_to_all(out, "dom", 0, 0, tiled=True, axis_index_groups=along_z)

    return call(
        scatter_kernel,
        (shape((width, nodes_dev), F32), shape((width, TILE), F32), shape((width, TILE), F32)),
        [VMEM] * 4,
        got,
        hot,
        part,
        base,
    )


def solution(mesh):
    return jax.shard_map(
        body,
        mesh=mesh,
        in_specs=(
            P("feat", "dom"),
            P("feat", "dom"),
            P("feat", "dom"),
            P("feat", "dom"),
            P("feat", None),
            P("feat", None),
            P("dom", None, None),
            P("dom"),
            P("dom"),
            P("dom"),
            P("dom", None, None),
            P("dom", None),
        ),
        out_specs=(P("feat", "dom"), P("feat", None), P("feat", None)),
        check_vma=False,
    )
```

```python
import jax
import jax.numpy as jnp
from jax import lax
from jax.experimental import pallas as pl
from jax.experimental.pallas import tpu as pltpu
from jax.sharding import PartitionSpec as P

TILE = 128
Y = 4
F32 = jnp.float32
BF16 = jnp.bfloat16
NT = (((1,), (1,)), ((), ()))
VMEM = pl.BlockSpec(memory_space=pltpu.VMEM)
ANY = pl.BlockSpec(memory_space=pl.ANY)
SMEM = pl.BlockSpec(memory_space=pltpu.SMEM)
MIB = 1024 * 1024
CHUNKS = 4


FEAT_ORDER = [3, 4, 5, 6, 7, 0, 1, 2]
Y_ORDER = [2, 3, 0, 1]
Z_ORDER = [10, 8, 9, 7, 0, 1, 2, 15, 3, 14, 4, 13, 5, 12, 6, 11]


def split(x):
    high = x.astype(BF16)
    return high, (x - high.astype(F32)).astype(BF16)


def press(x):
    square = x * 2.0**14
    square = square * square
    return jnp.where(x < 0, -square * square, square * square).astype(BF16)


def release(x):
    x = x.astype(F32)
    root = jnp.sqrt(jnp.sqrt(jnp.abs(x))) * 2.0**-14
    return jnp.where(x < 0, -root, jnp.where(x > 0, root, 0.0))


def fetch(pairs, sems):
    copies = [pltpu.make_async_copy(src, dst, sems.at[i]) for i, (src, dst) in enumerate(pairs)]
    for copy in copies:
        copy.start()
    return copies


def gate_kernel(preact, grad_out, out, gate, grad, sems):
    for copy in fetch([(preact, gate), (grad_out, grad)], sems):
        copy.wait()
    dz = jnp.where(gate[...] > 0, grad[...], jnp.zeros_like(grad))
    for copy in range(out.shape[0]):
        out[copy] = dz


def prep_kernel(count, target, tiles_in, tiles, degree, sems):
    step = tiles.shape[0] // CHUNKS
    spans = [pl.ds(i * step, step) for i in range(CHUNKS)]
    copies = fetch([(tiles_in.at[span], tiles.at[span]) for span in spans], sems)
    degree[...] = jnp.zeros_like(degree)
    ones = jnp.ones((8, TILE), BF16)
    for i, copy in enumerate(copies):
        copy.wait()
        for k in range(i * step, (i + 1) * step):
            sums = lax.dot_general(ones, tiles[k], NT, preferred_element_type=F32)
            degree[target[k]] += jnp.where(k < count[0], sums, 0.0)
    degree[...] = jnp.maximum(degree[...], 1.0)


def route_kernel(recv_rows, recv_count, hot, part, rows, counts, sems):
    for copy in fetch([(recv_rows.at[0], rows), (recv_count.at[0], counts)], sems):
        copy.wait()
    nz = rows.shape[0] // Y
    slots = rows.shape[1]
    lane = lax.broadcasted_iota(jnp.int32, (1, slots), 1)
    sub = lax.broadcasted_iota(jnp.int32, (TILE, TILE), 0)
    for z in range(nz):
        for m in range(Y // 2):
            pair = []
            for y in (2 * m, 2 * m + 1):
                s = y * nz + z
                pair.append(jnp.where(lane < counts[s], rows[s : s + 1], -1))
            row = jnp.concatenate(pair, axis=1)
            k = (z * (Y // 2) + m) * TILE
            hot[:, k : k + TILE] = (jnp.broadcast_to(row & (TILE - 1), (TILE, TILE)) == sub).astype(F32).astype(BF16)
            part[:, k : k + TILE] = jnp.broadcast_to(row >> 7, (16, TILE)).astype(F32).astype(BF16)


def tile_kernel(count, target, source, dz, packed, tiles, degree, out, base, messages, sums):
    tiles_dev = messages.shape[0]
    halo = sums.shape[0] - tiles_dev
    per = halo // Y
    places = [FEAT_ORDER.index(f) * 16 for f in range(len(FEAT_ORDER))]
    dz = jnp.concatenate([dz[p : p + 16] for p in places], axis=0)
    high, low = split(lax.dot_general(packed[:, : dz.shape[1]], dz, NT, preferred_element_type=F32))
    rows = high.shape[0]
    for y in range(Y):
        out[y, per * 16 : per * 16 + rows] = high
        out[y, per * 16 + rows : per * 16 + 2 * rows] = low
    product = jnp.dot(packed[:, dz.shape[1] :], dz, preferred_element_type=F32)
    for t in range(tiles_dev):
        columns = slice(t * TILE, (t + 1) * TILE)
        messages[t] = (product[:16, columns] / degree[t, 0:1]).astype(BF16)
    sums[...] = jnp.zeros_like(sums)
    for k in range(tiles.shape[0]):
        block = messages[target[k]]
        block = jnp.where(k < count[0], block, jnp.zeros_like(block))
        sums[source[k]] += jnp.dot(block, tiles[k], preferred_element_type=F32)
    for t in range(tiles_dev):
        columns = slice(t * TILE, (t + 1) * TILE)
        base[:, columns] = product[16:, columns] + sums[t]
    for b in range(halo):
        out[Y_ORDER.index(b // per), (b % per) * 16 : (b % per + 1) * 16] = sums[tiles_dev + b].astype(BF16)


def repack_kernel(got, out):
    nz, rows = out.shape[0], 32
    per = nz // 2
    total = jnp.zeros((rows, TILE), F32)
    for y in range(Y):
        total += got[y, per * 16 : per * 16 + rows].astype(F32)
        total += got[y, per * 16 + rows : per * 16 + 2 * rows].astype(F32)
    sent = press(total)
    first = lax.broadcasted_iota(jnp.int32, (16, TILE), 1) < TILE // 2
    for pair in range(per):
        for m in range(Y // 2):
            a = got[Y_ORDER.index(2 * m), pair * 16 : (pair + 1) * 16].astype(F32)
            b = got[Y_ORDER.index(2 * m + 1), pair * 16 : (pair + 1) * 16].astype(F32)
            out[Z_ORDER.index(2 * pair), m * 16 : (m + 1) * 16] = jnp.where(first, a, pltpu.roll(b, TILE // 2, 1)).astype(BF16)
            out[Z_ORDER.index(2 * pair + 1), m * 16 : (m + 1) * 16] = jnp.where(first, pltpu.roll(a, TILE // 2, 1), b).astype(BF16)
    for z in range(nz):
        out[z, Y * 8 : Y * 8 + rows] = sent


def scatter_kernel(got, hot, part, base, out, grad_w_self, grad_w_neigh):
    nz, rows = got.shape[0], 32
    tiles_dev = base.shape[1] // TILE
    total = jnp.zeros((tiles_dev * 16, TILE), F32)
    weight = jnp.zeros((rows, TILE), F32)
    for z in range(nz):
        values = jnp.concatenate([got[Z_ORDER.index(z), m * 16 : (m + 1) * 16] for m in range(Y // 2)], axis=1)
        span = slice(z * values.shape[1], (z + 1) * values.shape[1])
        where = part[:, span]
        spread = jnp.concatenate([jnp.where(where == t, values, jnp.zeros_like(values)) for t in range(tiles_dev)], axis=0)
        total += lax.dot_general(spread, hot[:, span], NT, preferred_element_type=F32)
        weight += release(got[z, Y * 8 : Y * 8 + rows])
    for t in range(tiles_dev):
        columns = slice(t * TILE, (t + 1) * TILE)
        out[:, columns] = base[:, columns] + total[t * 16 : (t + 1) * 16]
    grad_w_self[...] = weight[:16]
    grad_w_neigh[...] = weight[16:]


def call(kernel, outs, specs, *args, scratch=(), moved=0, limit=48):
    return pl.pallas_call(
        kernel,
        out_shape=outs,
        in_specs=specs,
        out_specs=jax.tree.map(lambda _: VMEM, outs),
        scratch_shapes=scratch,
        compiler_params=pltpu.CompilerParams(vmem_limit_bytes=limit * MIB),
        cost_estimate=pl.CostEstimate(flops=0, bytes_accessed=moved, transcendentals=0),
    )(*args)


def body(
    feats,
    aggregated,
    preact,
    grad_out,
    w_self,
    w_neigh,
    tile_values,
    tile_target,
    tile_source,
    tile_count,
    recv_rows,
    recv_count,
):
    width, nodes_dev = feats.shape
    ndom = lax.axis_size("dom")
    nfeat = lax.axis_size("feat")
    slots = recv_rows.shape[2]
    tiles_dev = nodes_dev // TILE
    halo_tiles = ndom * slots // TILE
    nz = ndom // Y
    along_y = [[y * nz + z for y in Y_ORDER] for z in range(nz)]
    along_z = [[y * nz + z for z in Z_ORDER] for y in range(Y)]
    shape = jax.ShapeDtypeStruct

    dz = call(
        gate_kernel,
        shape((nfeat, width, nodes_dev), BF16),
        [ANY] * 2,
        preact,
        grad_out,
        scratch=[pltpu.VMEM((width, nodes_dev), BF16)] * 2 + [pltpu.SemaphoreType.DMA((2,))],
        limit=60,
    )
    dz = lax.all_to_all(dz, "feat", 0, 0, tiled=True, axis_index_groups=[FEAT_ORDER]).reshape(nfeat * width, nodes_dev)
    packed = jnp.concatenate(
        [jnp.concatenate([feats, w_neigh], axis=1), jnp.concatenate([aggregated, w_self], axis=1)], axis=0
    )
    tiles, degree = call(
        prep_kernel,
        (shape(tile_values.shape, BF16), shape((tiles_dev, 8, TILE), F32)),
        [SMEM] * 2 + [ANY],
        tile_count,
        tile_target,
        tile_values,
        scratch=[pltpu.SemaphoreType.DMA((CHUNKS,))],
        moved=4000000,
        limit=51,
    )
    hot, part = call(
        route_kernel,
        (shape((TILE, ndom * slots), BF16), shape((16, ndom * slots), BF16)),
        [ANY] * 2,
        recv_rows,
        recv_count,
        scratch=[
            pltpu.VMEM((ndom, slots), jnp.int32),
            pltpu.SMEM((ndom,), jnp.int32),
            pltpu.SemaphoreType.DMA((2,)),
        ],
        moved=4000000,
    )

    per = halo_tiles // Y
    out, base = call(
        tile_kernel,
        (shape((Y, per * 16 + 4 * width, TILE), BF16), shape((width, nodes_dev), F32)),
        [SMEM] * 3 + [VMEM] * 4,
        tile_count,
        tile_target,
        tile_source,
        dz,
        packed,
        tiles,
        degree,
        scratch=[pltpu.VMEM((tiles_dev, width, TILE), BF16), pltpu.VMEM((tiles_dev + halo_tiles, width, TILE), F32)],
    )
    got = lax.all_to_all(out, "dom", 0, 0, tiled=True, axis_index_groups=along_y)
    out = call(repack_kernel, shape((nz, Y * 8 + 2 * width, TILE), BF16), [VMEM], got)
    got = lax.all_to_all(out, "dom", 0, 0, tiled=True, axis_index_groups=along_z)

    return call(
        scatter_kernel,
        (shape((width, nodes_dev), F32), shape((width, TILE), F32), shape((width, TILE), F32)),
        [VMEM] * 4,
        got,
        hot,
        part,
        base,
    )


def solution(mesh):
    return jax.shard_map(
        body,
        mesh=mesh,
        in_specs=(
            P("feat", "dom"),
            P("feat", "dom"),
            P("feat", "dom"),
            P("feat", "dom"),
            P("feat", None),
            P("feat", None),
            P("dom", None, None),
            P("dom"),
            P("dom"),
            P("dom"),
            P("dom", None, None),
            P("dom", None),
        ),
        out_specs=(P("feat", "dom"), P("feat", None), P("feat", None)),
        check_vma=False,
    )
```

```python
import jax
import jax.numpy as jnp
from jax import lax
from jax.experimental import pallas as pl
from jax.experimental.pallas import tpu as pltpu
from jax.sharding import PartitionSpec as P

TILE = 128
Y = 4
F32 = jnp.float32
BF16 = jnp.bfloat16
NT = (((1,), (1,)), ((), ()))
VMEM = pl.BlockSpec(memory_space=pltpu.VMEM)
ANY = pl.BlockSpec(memory_space=pl.ANY)
SMEM = pl.BlockSpec(memory_space=pltpu.SMEM)
MIB = 1024 * 1024
CHUNKS = 4


FEAT_ORDER = [3, 4, 5, 6, 7, 0, 1, 2]
NEAR_ORDER = [(2, 1), (2, 0), (3, 1), (3, 0), (0, 1), (0, 0), (1, 1), (1, 0)]
FAR_ORDER = [4, 5, 6, 7, 0, 1, 2, 3]


def split(x):
    high = x.astype(BF16)
    return high, (x - high.astype(F32)).astype(BF16)


def press(x):
    square = x * 2.0**14
    square = square * square
    return jnp.where(x < 0, -square * square, square * square).astype(BF16)


def release(x):
    x = x.astype(F32)
    root = jnp.sqrt(jnp.sqrt(jnp.abs(x))) * 2.0**-14
    return jnp.where(x < 0, -root, jnp.where(x > 0, root, 0.0))


def fetch(pairs, sems):
    copies = [pltpu.make_async_copy(src, dst, sems.at[i]) for i, (src, dst) in enumerate(pairs)]
    for copy in copies:
        copy.start()
    return copies


def gate_kernel(preact, grad_out, out, gate, grad, sems):
    for copy in fetch([(preact, gate), (grad_out, grad)], sems):
        copy.wait()
    dz = jnp.where(gate[...] > 0, grad[...], jnp.zeros_like(grad))
    for copy in range(out.shape[0]):
        out[copy] = dz


def prep_kernel(count, target, tiles_in, tiles, degree, sems):
    step = tiles.shape[0] // CHUNKS
    spans = [pl.ds(i * step, step) for i in range(CHUNKS)]
    copies = fetch([(tiles_in.at[span], tiles.at[span]) for span in spans], sems)
    degree[...] = jnp.zeros_like(degree)
    ones = jnp.ones((8, TILE), BF16)
    for i, copy in enumerate(copies):
        copy.wait()
        for k in range(i * step, (i + 1) * step):
            sums = lax.dot_general(ones, tiles[k], NT, preferred_element_type=F32)
            degree[target[k]] += jnp.where(k < count[0], sums, 0.0)
    degree[...] = jnp.maximum(degree[...], 1.0)


def route_kernel(recv_rows, recv_count, hot, part, rows, counts, sems):
    for copy in fetch([(recv_rows.at[0], rows), (recv_count.at[0], counts)], sems):
        copy.wait()
    slots = rows.shape[1]
    lane = lax.broadcasted_iota(jnp.int32, (1, slots), 1)
    sub = lax.broadcasted_iota(jnp.int32, (TILE, TILE), 0)
    for pair in range(rows.shape[0] // 2):
        halves = [jnp.where(lane < counts[s], rows[s : s + 1], -1) for s in (2 * pair, 2 * pair + 1)]
        row = jnp.concatenate(halves, axis=1)
        k = pair * TILE
        hot[:, k : k + TILE] = (jnp.broadcast_to(row & (TILE - 1), (TILE, TILE)) == sub).astype(F32).astype(BF16)
        part[:, k : k + TILE] = jnp.broadcast_to(row >> 7, (16, TILE)).astype(F32).astype(BF16)


def exchange_halves(a, b):
    first = lax.broadcasted_iota(jnp.int32, a.shape, 1) < TILE // 2
    low = jnp.where(first, a, pltpu.roll(b, TILE // 2, 1))
    return low.astype(BF16), jnp.where(first, pltpu.roll(a, TILE // 2, 1), b).astype(BF16)


def tile_kernel(count, target, source, dz, packed, tiles, degree, out, base, messages, sums):
    tiles_dev = messages.shape[0]
    per = (sums.shape[0] - tiles_dev) // Y
    body_rows = per * 8
    places = [FEAT_ORDER.index(f) * 16 for f in range(len(FEAT_ORDER))]
    dz = jnp.concatenate([dz[p : p + 16] for p in places], axis=0)
    sent = press(lax.dot_general(packed[:, : dz.shape[1]], dz, NT, preferred_element_type=F32))
    for peer in range(out.shape[0]):
        out[peer, body_rows:] = sent
    product = jnp.dot(packed[:, dz.shape[1] :], dz, preferred_element_type=F32)
    for t in range(tiles_dev):
        columns = slice(t * TILE, (t + 1) * TILE)
        messages[t] = (product[:16, columns] / degree[t, 0:1]).astype(BF16)
    sums[...] = jnp.zeros_like(sums)
    for k in range(tiles.shape[0]):
        block = messages[target[k]]
        block = jnp.where(k < count[0], block, jnp.zeros_like(block))
        sums[source[k]] += jnp.dot(block, tiles[k], preferred_element_type=F32)
    for t in range(tiles_dev):
        columns = slice(t * TILE, (t + 1) * TILE)
        base[:, columns] = product[16:, columns] + sums[t]
    for y in range(Y):
        for q in range(per // 2):
            block = tiles_dev + y * per + 2 * q
            even, odd = exchange_halves(sums[block], sums[block + 1])
            out[NEAR_ORDER.index((y, 0)), q * 16 : (q + 1) * 16] = even
            out[NEAR_ORDER.index((y, 1)), q * 16 : (q + 1) * 16] = odd


def repack_kernel(got, out):
    pairs = out.shape[0]
    body_rows = pairs * 8
    total = jnp.zeros((got.shape[1] - body_rows, TILE), F32)
    for peer in range(got.shape[0]):
        total += release(got[peer, body_rows:])
    sent = press(total)
    for peer in range(pairs):
        out[peer, Y * 16 :] = sent
    for y in range(Y):
        for q in range(pairs // 2):
            a = got[NEAR_ORDER.index((y, 0)), q * 16 : (q + 1) * 16].astype(F32)
            b = got[NEAR_ORDER.index((y, 1)), q * 16 : (q + 1) * 16].astype(F32)
            low, high = exchange_halves(a, b)
            out[FAR_ORDER.index(2 * q), y * 16 : (y + 1) * 16] = low
            out[FAR_ORDER.index(2 * q + 1), y * 16 : (y + 1) * 16] = high


def scatter_kernel(got, hot, part, base, out, grad_w_self, grad_w_neigh):
    pairs = got.shape[0]
    tiles_dev = base.shape[1] // TILE
    total = jnp.zeros((tiles_dev * 16, TILE), F32)
    weight = jnp.zeros((got.shape[1] - Y * 16, TILE), F32)
    for y in range(Y):
        for p in range(0, pairs, 2):
            values = jnp.concatenate([got[FAR_ORDER.index(c), y * 16 : (y + 1) * 16] for c in (p, p + 1)], axis=1)
            k = (y * pairs + p) * TILE
            span = slice(k, k + 2 * TILE)
            where = part[:, span]
            spread = jnp.concatenate([jnp.where(where == t, values, jnp.zeros_like(values)) for t in range(tiles_dev)], axis=0)
            total += lax.dot_general(spread, hot[:, span], NT, preferred_element_type=F32)
    for peer in range(pairs):
        weight += release(got[peer, Y * 16 :])
    for t in range(tiles_dev):
        columns = slice(t * TILE, (t + 1) * TILE)
        out[:, columns] = base[:, columns] + total[t * 16 : (t + 1) * 16]
    grad_w_self[...] = weight[:16]
    grad_w_neigh[...] = weight[16:]


def call(kernel, outs, specs, *args, scratch=(), moved=0, limit=48):
    return pl.pallas_call(
        kernel,
        out_shape=outs,
        in_specs=specs,
        out_specs=jax.tree.map(lambda _: VMEM, outs),
        scratch_shapes=scratch,
        compiler_params=pltpu.CompilerParams(vmem_limit_bytes=limit * MIB),
        cost_estimate=pl.CostEstimate(flops=0, bytes_accessed=moved, transcendentals=0),
    )(*args)


def body(
    feats,
    aggregated,
    preact,
    grad_out,
    w_self,
    w_neigh,
    tile_values,
    tile_target,
    tile_source,
    tile_count,
    recv_rows,
    recv_count,
):
    width, nodes_dev = feats.shape
    ndom = lax.axis_size("dom")
    nfeat = lax.axis_size("feat")
    slots = recv_rows.shape[2]
    tiles_dev = nodes_dev // TILE
    halo_tiles = ndom * slots // TILE
    nz = ndom // Y
    pairs = nz // 2
    near = [[y * nz + 2 * p + odd for y, odd in NEAR_ORDER] for p in range(pairs)]
    far = [[y * nz + 2 * p + odd for p in FAR_ORDER] for y in range(Y) for odd in range(2)]
    shape = jax.ShapeDtypeStruct

    dz = call(
        gate_kernel,
        shape((nfeat, width, nodes_dev), BF16),
        [ANY] * 2,
        preact,
        grad_out,
        scratch=[pltpu.VMEM((width, nodes_dev), BF16)] * 2 + [pltpu.SemaphoreType.DMA((2,))],
        limit=60,
    )
    dz = lax.all_to_all(dz, "feat", 0, 0, tiled=True, axis_index_groups=[FEAT_ORDER]).reshape(nfeat * width, nodes_dev)
    packed = jnp.concatenate(
        [jnp.concatenate([feats, w_neigh], axis=1), jnp.concatenate([aggregated, w_self], axis=1)], axis=0
    )
    tiles, degree = call(
        prep_kernel,
        (shape(tile_values.shape, BF16), shape((tiles_dev, 8, TILE), F32)),
        [SMEM] * 2 + [ANY],
        tile_count,
        tile_target,
        tile_values,
        scratch=[pltpu.SemaphoreType.DMA((CHUNKS,))],
        moved=4000000,
        limit=51,
    )
    hot, part = call(
        route_kernel,
        (shape((TILE, ndom * slots), BF16), shape((16, ndom * slots), BF16)),
        [ANY] * 2,
        recv_rows,
        recv_count,
        scratch=[
            pltpu.VMEM((ndom, slots), jnp.int32),
            pltpu.SMEM((ndom,), jnp.int32),
            pltpu.SemaphoreType.DMA((2,)),
        ],
        moved=4000000,
    )

    out, base = call(
        tile_kernel,
        (shape((2 * Y, pairs * 8 + 2 * width, TILE), BF16), shape((width, nodes_dev), F32)),
        [SMEM] * 3 + [VMEM] * 4,
        tile_count,
        tile_target,
        tile_source,
        dz,
        packed,
        tiles,
        degree,
        scratch=[pltpu.VMEM((tiles_dev, width, TILE), BF16), pltpu.VMEM((tiles_dev + halo_tiles, width, TILE), F32)],
    )
    got = lax.all_to_all(out, "dom", 0, 0, tiled=True, axis_index_groups=near)
    out = call(repack_kernel, shape((pairs, Y * 16 + 2 * width, TILE), BF16), [VMEM], got)
    got = lax.all_to_all(out, "dom", 0, 0, tiled=True, axis_index_groups=far)
    return call(
        scatter_kernel,
        (shape((width, nodes_dev), F32), shape((width, TILE), F32), shape((width, TILE), F32)),
        [VMEM] * 4,
        got,
        hot,
        part,
        base,
    )


def solution(mesh):
    return jax.shard_map(
        body,
        mesh=mesh,
        in_specs=(
            P("feat", "dom"),
            P("feat", "dom"),
            P("feat", "dom"),
            P("feat", "dom"),
            P("feat", None),
            P("feat", None),
            P("dom", None, None),
            P("dom"),
            P("dom"),
            P("dom"),
            P("dom", None, None),
            P("dom", None),
        ),
        out_specs=(P("feat", "dom"), P("feat", None), P("feat", None)),
        check_vma=False,
    )
```

```python
import jax
import jax.numpy as jnp
from jax import lax
from jax.experimental import pallas as pl
from jax.experimental.pallas import tpu as pltpu
from jax.sharding import PartitionSpec as P

TILE = 128
Y = 4
F32 = jnp.float32
BF16 = jnp.bfloat16
NT = (((1,), (1,)), ((), ()))
VMEM = pl.BlockSpec(memory_space=pltpu.VMEM)
ANY = pl.BlockSpec(memory_space=pl.ANY)
SMEM = pl.BlockSpec(memory_space=pltpu.SMEM)
MIB = 1024 * 1024
CHUNKS = 4


FEAT_ORDER = [3, 4, 5, 6, 7, 0, 1, 2]
NEAR_ORDER = [(2, 1), (2, 0), (3, 1), (3, 0), (0, 1), (0, 0), (1, 1), (1, 0)]
FAR_ORDER = [5, 0, 4, 1, 6, 7, 3, 2]


def split(x):
    high = x.astype(BF16)
    return high, (x - high.astype(F32)).astype(BF16)


def press(x):
    square = x * 2.0**13
    square = square * square
    return jnp.where(x < 0, -square * square, square * square).astype(BF16)


def release(x):
    x = x.astype(F32)
    root = jnp.sqrt(jnp.sqrt(jnp.abs(x))) * 2.0**-13
    return jnp.where(x < 0, -root, jnp.where(x > 0, root, 0.0))


def fetch(pairs, sems):
    copies = [pltpu.make_async_copy(src, dst, sems.at[i]) for i, (src, dst) in enumerate(pairs)]
    for copy in copies:
        copy.start()
    return copies


def gate_kernel(preact, grad_out, out, gate, grad, sems):
    for copy in fetch([(preact, gate), (grad_out, grad)], sems):
        copy.wait()
    dz = jnp.where(gate[...] > 0, grad[...], jnp.zeros_like(grad))
    for copy in range(out.shape[0]):
        out[copy] = dz


def prep_kernel(count, target, tiles_in, tiles, degree, sems):
    step = tiles.shape[0] // CHUNKS
    spans = [pl.ds(i * step, step) for i in range(CHUNKS)]
    copies = fetch([(tiles_in.at[span], tiles.at[span]) for span in spans], sems)
    degree[...] = jnp.zeros_like(degree)
    ones = jnp.ones((8, TILE), BF16)
    for i, copy in enumerate(copies):
        copy.wait()
        for k in range(i * step, (i + 1) * step):
            sums = lax.dot_general(ones, tiles[k], NT, preferred_element_type=F32)
            degree[target[k]] += jnp.where(k < count[0], sums, 0.0)
    degree[...] = jnp.maximum(degree[...], 1.0)


def route_kernel(recv_rows, recv_count, hot, part, rows, counts, sems):
    for copy in fetch([(recv_rows.at[0], rows), (recv_count.at[0], counts)], sems):
        copy.wait()
    slots = rows.shape[1]
    lane = lax.broadcasted_iota(jnp.int32, (1, slots), 1)
    sub = lax.broadcasted_iota(jnp.int32, (TILE, TILE), 0)
    for pair in range(rows.shape[0] // 2):
        halves = [jnp.where(lane < counts[s], rows[s : s + 1], -1) for s in (2 * pair, 2 * pair + 1)]
        row = jnp.concatenate(halves, axis=1)
        k = pair * TILE
        hot[:, k : k + TILE] = (jnp.broadcast_to(row & (TILE - 1), (TILE, TILE)) == sub).astype(F32).astype(BF16)
        part[:, k : k + TILE] = jnp.broadcast_to(row >> 7, (16, TILE)).astype(F32).astype(BF16)


def exchange_halves(a, b):
    first = lax.broadcasted_iota(jnp.int32, a.shape, 1) < TILE // 2
    low = jnp.where(first, a, pltpu.roll(b, TILE // 2, 1))
    return low.astype(BF16), jnp.where(first, pltpu.roll(a, TILE // 2, 1), b).astype(BF16)


def tile_kernel(count, target, source, dz, packed, tiles, degree, out, base, messages, sums):
    tiles_dev = messages.shape[0]
    per = (sums.shape[0] - tiles_dev) // Y
    body_rows = per * 8
    places = [FEAT_ORDER.index(f) * 16 for f in range(len(FEAT_ORDER))]
    dz = jnp.concatenate([dz[p : p + 16] for p in places], axis=0)
    sent = press(lax.dot_general(packed[:, : dz.shape[1]], dz, NT, preferred_element_type=F32))
    for peer in range(out.shape[0]):
        out[peer, body_rows:] = sent
    product = jnp.dot(packed[:, dz.shape[1] :], dz, preferred_element_type=F32)
    for t in range(tiles_dev):
        columns = slice(t * TILE, (t + 1) * TILE)
        messages[t] = (product[:16, columns] / degree[t, 0:1]).astype(BF16)
    sums[...] = jnp.zeros_like(sums)
    for k in range(tiles.shape[0]):
        block = messages[target[k]]
        block = jnp.where(k < count[0], block, jnp.zeros_like(block))
        sums[source[k]] += jnp.dot(block, tiles[k], preferred_element_type=F32)
    for t in range(tiles_dev):
        columns = slice(t * TILE, (t + 1) * TILE)
        base[:, columns] = product[16:, columns] + sums[t]
    for y in range(Y):
        for q in range(per // 2):
            block = tiles_dev + y * per + 2 * q
            even, odd = exchange_halves(sums[block], sums[block + 1])
            out[NEAR_ORDER.index((y, 0)), q * 16 : (q + 1) * 16] = even
            out[NEAR_ORDER.index((y, 1)), q * 16 : (q + 1) * 16] = odd


def repack_kernel(got, out):
    pairs = out.shape[0]
    body_rows = pairs * 8
    total = jnp.zeros((got.shape[1] - body_rows, TILE), F32)
    for peer in range(got.shape[0]):
        total += release(got[peer, body_rows:])
    sent = press(total)
    for peer in range(pairs):
        out[peer, Y * 16 :] = sent
    for y in range(Y):
        for q in range(pairs // 2):
            a = got[NEAR_ORDER.index((y, 0)), q * 16 : (q + 1) * 16].astype(F32)
            b = got[NEAR_ORDER.index((y, 1)), q * 16 : (q + 1) * 16].astype(F32)
            low, high = exchange_halves(a, b)
            out[FAR_ORDER.index(2 * q), y * 16 : (y + 1) * 16] = low
            out[FAR_ORDER.index(2 * q + 1), y * 16 : (y + 1) * 16] = high


def scatter_kernel(got, hot, part, base, out, grad_w_self, grad_w_neigh):
    pairs = got.shape[0]
    tiles_dev = base.shape[1] // TILE
    total = jnp.zeros((tiles_dev * 16, TILE), F32)
    weight = jnp.zeros((got.shape[1] - Y * 16, TILE), F32)
    for y in range(Y):
        for p in range(0, pairs, 2):
            values = jnp.concatenate([got[FAR_ORDER.index(c), y * 16 : (y + 1) * 16] for c in (p, p + 1)], axis=1)
            k = (y * pairs + p) * TILE
            span = slice(k, k + 2 * TILE)
            where = part[:, span]
            spread = jnp.concatenate([jnp.where(where == t, values, jnp.zeros_like(values)) for t in range(tiles_dev)], axis=0)
            total += lax.dot_general(spread, hot[:, span], NT, preferred_element_type=F32)
    for peer in range(pairs):
        weight += release(got[peer, Y * 16 :])
    for t in range(tiles_dev):
        columns = slice(t * TILE, (t + 1) * TILE)
        out[:, columns] = base[:, columns] + total[t * 16 : (t + 1) * 16]
    grad_w_self[...] = weight[:16]
    grad_w_neigh[...] = weight[16:]


def call(kernel, outs, specs, *args, scratch=(), moved=0, limit=48):
    return pl.pallas_call(
        kernel,
        out_shape=outs,
        in_specs=specs,
        out_specs=jax.tree.map(lambda _: VMEM, outs),
        scratch_shapes=scratch,
        compiler_params=pltpu.CompilerParams(vmem_limit_bytes=limit * MIB),
        cost_estimate=pl.CostEstimate(flops=0, bytes_accessed=moved, transcendentals=0),
    )(*args)


def body(
    feats,
    aggregated,
    preact,
    grad_out,
    w_self,
    w_neigh,
    tile_values,
    tile_target,
    tile_source,
    tile_count,
    recv_rows,
    recv_count,
):
    width, nodes_dev = feats.shape
    ndom = lax.axis_size("dom")
    nfeat = lax.axis_size("feat")
    slots = recv_rows.shape[2]
    tiles_dev = nodes_dev // TILE
    halo_tiles = ndom * slots // TILE
    nz = ndom // Y
    pairs = nz // 2
    near = [[y * nz + 2 * p + odd for y, odd in NEAR_ORDER] for p in range(pairs)]
    far = [[y * nz + 2 * p + odd for p in FAR_ORDER] for y in range(Y) for odd in range(2)]
    shape = jax.ShapeDtypeStruct

    dz = call(
        gate_kernel,
        shape((nfeat, width, nodes_dev), BF16),
        [ANY] * 2,
        preact,
        grad_out,
        scratch=[pltpu.VMEM((width, nodes_dev), BF16)] * 2 + [pltpu.SemaphoreType.DMA((2,))],
        limit=60,
    )
    dz = lax.all_to_all(dz, "feat", 0, 0, tiled=True, axis_index_groups=[FEAT_ORDER]).reshape(nfeat * width, nodes_dev)
    packed = jnp.concatenate(
        [jnp.concatenate([feats, w_neigh], axis=1), jnp.concatenate([aggregated, w_self], axis=1)], axis=0
    )
    tiles, degree = call(
        prep_kernel,
        (shape(tile_values.shape, BF16), shape((tiles_dev, 8, TILE), F32)),
        [SMEM] * 2 + [ANY],
        tile_count,
        tile_target,
        tile_values,
        scratch=[pltpu.SemaphoreType.DMA((CHUNKS,))],
        moved=4000000,
        limit=51,
    )
    hot, part = call(
        route_kernel,
        (shape((TILE, ndom * slots), BF16), shape((16, ndom * slots), BF16)),
        [ANY] * 2,
        recv_rows,
        recv_count,
        scratch=[
            pltpu.VMEM((ndom, slots), jnp.int32),
            pltpu.SMEM((ndom,), jnp.int32),
            pltpu.SemaphoreType.DMA((2,)),
        ],
        moved=4000000,
    )

    out, base = call(
        tile_kernel,
        (shape((2 * Y, pairs * 8 + 2 * width, TILE), BF16), shape((width, nodes_dev), F32)),
        [SMEM] * 3 + [VMEM] * 4,
        tile_count,
        tile_target,
        tile_source,
        dz,
        packed,
        tiles,
        degree,
        scratch=[pltpu.VMEM((tiles_dev, width, TILE), BF16), pltpu.VMEM((tiles_dev + halo_tiles, width, TILE), F32)],
    )
    got = lax.all_to_all(out, "dom", 0, 0, tiled=True, axis_index_groups=near)
    out = call(repack_kernel, shape((pairs, Y * 16 + 2 * width, TILE), BF16), [VMEM], got)
    got = lax.all_to_all(out, "dom", 0, 0, tiled=True, axis_index_groups=far)
    return call(
        scatter_kernel,
        (shape((width, nodes_dev), F32), shape((width, TILE), F32), shape((width, TILE), F32)),
        [VMEM] * 4,
        got,
        hot,
        part,
        base,
    )


def solution(mesh):
    return jax.shard_map(
        body,
        mesh=mesh,
        in_specs=(
            P("feat", "dom"),
            P("feat", "dom"),
            P("feat", "dom"),
            P("feat", "dom"),
            P("feat", None),
            P("feat", None),
            P("dom", None, None),
            P("dom"),
            P("dom"),
            P("dom"),
            P("dom", None, None),
            P("dom", None),
        ),
        out_specs=(P("feat", "dom"), P("feat", None), P("feat", None)),
        check_vma=False,
    )
```

```python
import jax
import jax.numpy as jnp
from jax import lax
from jax.experimental import pallas as pl
from jax.experimental.pallas import tpu as pltpu
from jax.sharding import PartitionSpec as P

TILE = 128
Y = 4
F32 = jnp.float32
BF16 = jnp.bfloat16
NT = (((1,), (1,)), ((), ()))
VMEM = pl.BlockSpec(memory_space=pltpu.VMEM)
ANY = pl.BlockSpec(memory_space=pl.ANY)
SMEM = pl.BlockSpec(memory_space=pltpu.SMEM)
MIB = 1024 * 1024
CHUNKS = 4


FEAT_ORDER = [3, 4, 5, 6, 7, 0, 1, 2]
NEAR_ORDER = [(2, 1), (2, 0), (3, 1), (3, 0), (0, 1), (0, 0), (1, 1), (1, 0)]
FAR_ORDER = [5, 3, 0, 4, 1, 7, 6, 2]


def split(x):
    high = x.astype(BF16)
    return high, (x - high.astype(F32)).astype(BF16)


def press(x):
    square = x * 2.0**13
    square = square * square
    return jnp.where(x < 0, -square * square, square * square).astype(BF16)


def release(x):
    x = x.astype(F32)
    root = jnp.sqrt(jnp.sqrt(jnp.abs(x))) * 2.0**-13
    return jnp.where(x < 0, -root, jnp.where(x > 0, root, 0.0))


def fetch(pairs, sems):
    copies = [pltpu.make_async_copy(src, dst, sems.at[i]) for i, (src, dst) in enumerate(pairs)]
    for copy in copies:
        copy.start()
    return copies


def gate_kernel(preact, grad_out, out, gate, grad, sems):
    for copy in fetch([(preact, gate), (grad_out, grad)], sems):
        copy.wait()
    dz = jnp.where(gate[...] > 0, grad[...], jnp.zeros_like(grad))
    for copy in range(out.shape[0]):
        out[copy] = dz


def prep_kernel(count, target, tiles_in, tiles, degree, sems):
    step = tiles.shape[0] // CHUNKS
    spans = [pl.ds(i * step, step) for i in range(CHUNKS)]
    copies = fetch([(tiles_in.at[span], tiles.at[span]) for span in spans], sems)
    degree[...] = jnp.zeros_like(degree)
    ones = jnp.ones((8, TILE), BF16)
    for i, copy in enumerate(copies):
        copy.wait()
        for k in range(i * step, (i + 1) * step):
            sums = lax.dot_general(ones, tiles[k], NT, preferred_element_type=F32)
            degree[target[k]] += jnp.where(k < count[0], sums, 0.0)
    degree[...] = jnp.maximum(degree[...], 1.0)


def route_kernel(recv_rows, recv_count, hot, part, rows, counts, sems):
    for copy in fetch([(recv_rows.at[0], rows), (recv_count.at[0], counts)], sems):
        copy.wait()
    slots = rows.shape[1]
    lane = lax.broadcasted_iota(jnp.int32, (1, slots), 1)
    sub = lax.broadcasted_iota(jnp.int32, (TILE, TILE), 0)
    for pair in range(rows.shape[0] // 2):
        halves = [jnp.where(lane < counts[s], rows[s : s + 1], -1) for s in (2 * pair, 2 * pair + 1)]
        row = jnp.concatenate(halves, axis=1)
        k = pair * TILE
        hot[:, k : k + TILE] = (jnp.broadcast_to(row & (TILE - 1), (TILE, TILE)) == sub).astype(F32).astype(BF16)
        part[:, k : k + TILE] = jnp.broadcast_to(row >> 7, (16, TILE)).astype(F32).astype(BF16)


def exchange_halves(a, b):
    first = lax.broadcasted_iota(jnp.int32, a.shape, 1) < TILE // 2
    low = jnp.where(first, a, pltpu.roll(b, TILE // 2, 1))
    return low.astype(BF16), jnp.where(first, pltpu.roll(a, TILE // 2, 1), b).astype(BF16)


def tile_kernel(count, target, source, dz, packed, tiles, degree, out, base, messages, sums):
    tiles_dev = messages.shape[0]
    per = (sums.shape[0] - tiles_dev) // Y
    body_rows = per * 8
    places = [FEAT_ORDER.index(f) * 16 for f in range(len(FEAT_ORDER))]
    dz = jnp.concatenate([dz[p : p + 16] for p in places], axis=0)
    sent = press(lax.dot_general(packed[:, : dz.shape[1]], dz, NT, preferred_element_type=F32))
    for peer in range(out.shape[0]):
        out[peer, body_rows:] = sent
    product = jnp.dot(packed[:, dz.shape[1] :], dz, preferred_element_type=F32)
    for t in range(tiles_dev):
        columns = slice(t * TILE, (t + 1) * TILE)
        messages[t] = (product[:16, columns] / degree[t, 0:1]).astype(BF16)
    sums[...] = jnp.zeros_like(sums)
    for k in range(tiles.shape[0]):
        block = messages[target[k]]
        block = jnp.where(k < count[0], block, jnp.zeros_like(block))
        sums[source[k]] += jnp.dot(block, tiles[k], preferred_element_type=F32)
    for t in range(tiles_dev):
        columns = slice(t * TILE, (t + 1) * TILE)
        base[:, columns] = product[16:, columns] + sums[t]
    for y in range(Y):
        for q in range(per // 2):
            block = tiles_dev + y * per + 2 * q
            even, odd = exchange_halves(sums[block], sums[block + 1])
            out[NEAR_ORDER.index((y, 0)), q * 16 : (q + 1) * 16] = even
            out[NEAR_ORDER.index((y, 1)), q * 16 : (q + 1) * 16] = odd


def repack_kernel(got, out):
    pairs = out.shape[0]
    body_rows = pairs * 8
    total = jnp.zeros((got.shape[1] - body_rows, TILE), F32)
    for peer in range(got.shape[0]):
        total += release(got[peer, body_rows:])
    sent = press(total)
    for peer in range(pairs):
        out[peer, Y * 16 :] = sent
    for y in range(Y):
        for q in range(pairs // 2):
            a = got[NEAR_ORDER.index((y, 0)), q * 16 : (q + 1) * 16].astype(F32)
            b = got[NEAR_ORDER.index((y, 1)), q * 16 : (q + 1) * 16].astype(F32)
            low, high = exchange_halves(a, b)
            out[FAR_ORDER.index(2 * q), y * 16 : (y + 1) * 16] = low
            out[FAR_ORDER.index(2 * q + 1), y * 16 : (y + 1) * 16] = high


def scatter_kernel(got, hot, part, base, out, grad_w_self, grad_w_neigh):
    pairs = got.shape[0]
    tiles_dev = base.shape[1] // TILE
    total = jnp.zeros((tiles_dev * 16, TILE), F32)
    weight = jnp.zeros((got.shape[1] - Y * 16, TILE), F32)
    for y in range(Y):
        for p in range(0, pairs, 2):
            values = jnp.concatenate([got[FAR_ORDER.index(c), y * 16 : (y + 1) * 16] for c in (p, p + 1)], axis=1)
            k = (y * pairs + p) * TILE
            span = slice(k, k + 2 * TILE)
            where = part[:, span]
            spread = jnp.concatenate([jnp.where(where == t, values, jnp.zeros_like(values)) for t in range(tiles_dev)], axis=0)
            total += lax.dot_general(spread, hot[:, span], NT, preferred_element_type=F32)
    for peer in range(pairs):
        weight += release(got[peer, Y * 16 :])
    for t in range(tiles_dev):
        columns = slice(t * TILE, (t + 1) * TILE)
        out[:, columns] = base[:, columns] + total[t * 16 : (t + 1) * 16]
    grad_w_self[...] = weight[:16]
    grad_w_neigh[...] = weight[16:]


def call(kernel, outs, specs, *args, scratch=(), moved=0, limit=48):
    return pl.pallas_call(
        kernel,
        out_shape=outs,
        in_specs=specs,
        out_specs=jax.tree.map(lambda _: VMEM, outs),
        scratch_shapes=scratch,
        compiler_params=pltpu.CompilerParams(vmem_limit_bytes=limit * MIB),
        cost_estimate=pl.CostEstimate(flops=0, bytes_accessed=moved, transcendentals=0),
    )(*args)


def body(
    feats,
    aggregated,
    preact,
    grad_out,
    w_self,
    w_neigh,
    tile_values,
    tile_target,
    tile_source,
    tile_count,
    recv_rows,
    recv_count,
):
    width, nodes_dev = feats.shape
    ndom = lax.axis_size("dom")
    nfeat = lax.axis_size("feat")
    slots = recv_rows.shape[2]
    tiles_dev = nodes_dev // TILE
    halo_tiles = ndom * slots // TILE
    nz = ndom // Y
    pairs = nz // 2
    near = [[y * nz + 2 * p + odd for y, odd in NEAR_ORDER] for p in range(pairs)]
    far = [[y * nz + 2 * p + odd for p in FAR_ORDER] for y in range(Y) for odd in range(2)]
    shape = jax.ShapeDtypeStruct

    dz = call(
        gate_kernel,
        shape((nfeat, width, nodes_dev), BF16),
        [ANY] * 2,
        preact,
        grad_out,
        scratch=[pltpu.VMEM((width, nodes_dev), BF16)] * 2 + [pltpu.SemaphoreType.DMA((2,))],
        limit=60,
    )
    dz = lax.all_to_all(dz, "feat", 0, 0, tiled=True, axis_index_groups=[FEAT_ORDER]).reshape(nfeat * width, nodes_dev)
    packed = jnp.concatenate(
        [jnp.concatenate([feats, w_neigh], axis=1), jnp.concatenate([aggregated, w_self], axis=1)], axis=0
    )
    tiles, degree = call(
        prep_kernel,
        (shape(tile_values.shape, BF16), shape((tiles_dev, 8, TILE), F32)),
        [SMEM] * 2 + [ANY],
        tile_count,
        tile_target,
        tile_values,
        scratch=[pltpu.SemaphoreType.DMA((CHUNKS,))],
        moved=4000000,
        limit=51,
    )
    hot, part = call(
        route_kernel,
        (shape((TILE, ndom * slots), BF16), shape((16, ndom * slots), BF16)),
        [ANY] * 2,
        recv_rows,
        recv_count,
        scratch=[
            pltpu.VMEM((ndom, slots), jnp.int32),
            pltpu.SMEM((ndom,), jnp.int32),
            pltpu.SemaphoreType.DMA((2,)),
        ],
        moved=4000000,
    )

    out, base = call(
        tile_kernel,
        (shape((2 * Y, pairs * 8 + 2 * width, TILE), BF16), shape((width, nodes_dev), F32)),
        [SMEM] * 3 + [VMEM] * 4,
        tile_count,
        tile_target,
        tile_source,
        dz,
        packed,
        tiles,
        degree,
        scratch=[pltpu.VMEM((tiles_dev, width, TILE), BF16), pltpu.VMEM((tiles_dev + halo_tiles, width, TILE), F32)],
    )
    got = lax.all_to_all(out, "dom", 0, 0, tiled=True, axis_index_groups=near)
    out = call(repack_kernel, shape((pairs, Y * 16 + 2 * width, TILE), BF16), [VMEM], got)
    got = lax.all_to_all(out, "dom", 0, 0, tiled=True, axis_index_groups=far)
    return call(
        scatter_kernel,
        (shape((width, nodes_dev), F32), shape((width, TILE), F32), shape((width, TILE), F32)),
        [VMEM] * 4,
        got,
        hot,
        part,
        base,
    )


def solution(mesh):
    return jax.shard_map(
        body,
        mesh=mesh,
        in_specs=(
            P("feat", "dom"),
            P("feat", "dom"),
            P("feat", "dom"),
            P("feat", "dom"),
            P("feat", None),
            P("feat", None),
            P("dom", None, None),
            P("dom"),
            P("dom"),
            P("dom"),
            P("dom", None, None),
            P("dom", None),
        ),
        out_specs=(P("feat", "dom"), P("feat", None), P("feat", None)),
        check_vma=False,
    )
```

```python
import jax
import jax.numpy as jnp
from jax import lax
from jax.experimental import pallas as pl
from jax.experimental.pallas import tpu as pltpu
from jax.sharding import PartitionSpec as P

TILE = 128
Y = 4
F32 = jnp.float32
BF16 = jnp.bfloat16
NT = (((1,), (1,)), ((), ()))
VMEM = pl.BlockSpec(memory_space=pltpu.VMEM)
ANY = pl.BlockSpec(memory_space=pl.ANY)
SMEM = pl.BlockSpec(memory_space=pltpu.SMEM)
MIB = 1024 * 1024
CHUNKS = 4


FEAT_ORDER = [3, 4, 5, 6, 7, 0, 1, 2]
NEAR_ORDER = [(2, 1), (2, 0), (3, 1), (3, 0), (0, 1), (0, 0), (1, 1), (1, 0)]
FAR_ORDER = [5, 3, 0, 4, 1, 7, 6, 2]


def split(x):
    high = x.astype(BF16)
    return high, (x - high.astype(F32)).astype(BF16)


def press(x):
    square = x * 2.0**13
    square = square * square
    return jnp.where(x < 0, -square * square, square * square).astype(BF16)


def release(x):
    x = x.astype(F32)
    root = jnp.sqrt(jnp.sqrt(jnp.abs(x))) * 2.0**-13
    return jnp.where(x < 0, -root, jnp.where(x > 0, root, 0.0))


def fetch(pairs, sems):
    copies = [pltpu.make_async_copy(src, dst, sems.at[i]) for i, (src, dst) in enumerate(pairs)]
    for copy in copies:
        copy.start()
    return copies


def gate_kernel(preact, grad_out, out, gate, grad, sems):
    for copy in fetch([(preact, gate), (grad_out, grad)], sems):
        copy.wait()
    dz = jnp.where(gate[...] > 0, grad[...], jnp.zeros_like(grad))
    for copy in range(out.shape[0]):
        out[copy] = dz


def prep_kernel(count, target, tiles_in, tiles, degree, sems):
    step = tiles.shape[0] // CHUNKS
    spans = [pl.ds(i * step, step) for i in range(CHUNKS)]
    copies = fetch([(tiles_in.at[span], tiles.at[span]) for span in spans], sems)
    degree[...] = jnp.zeros_like(degree)
    ones = jnp.ones((8, TILE), BF16)
    for i, copy in enumerate(copies):
        copy.wait()
        for k in range(i * step, (i + 1) * step):
            sums = lax.dot_general(ones, tiles[k], NT, preferred_element_type=F32)
            degree[target[k]] += jnp.where(k < count[0], sums, 0.0)
    degree[...] = jnp.maximum(degree[...], 1.0)


def route_kernel(recv_rows, recv_count, hot, part, rows, counts, sems):
    for copy in fetch([(recv_rows.at[0], rows), (recv_count.at[0], counts)], sems):
        copy.wait()
    slots = rows.shape[1]
    lane = lax.broadcasted_iota(jnp.int32, (1, slots), 1)
    sub = lax.broadcasted_iota(jnp.int32, (TILE, TILE), 0)
    for pair in range(rows.shape[0] // 2):
        halves = [jnp.where(lane < counts[s], rows[s : s + 1], -1) for s in (2 * pair, 2 * pair + 1)]
        row = jnp.concatenate(halves, axis=1)
        k = pair * TILE
        hot[:, k : k + TILE] = (jnp.broadcast_to(row & (TILE - 1), (TILE, TILE)) == sub).astype(F32).astype(BF16)
        part[:, k : k + TILE] = jnp.broadcast_to(row >> 7, (16, TILE)).astype(F32).astype(BF16)


def exchange_halves(a, b):
    first = lax.broadcasted_iota(jnp.int32, a.shape, 1) < TILE // 2
    low = jnp.where(first, a, pltpu.roll(b, TILE // 2, 1))
    return low.astype(BF16), jnp.where(first, pltpu.roll(a, TILE // 2, 1), b).astype(BF16)


def tile_kernel(count, target, source, dz, packed, tiles, degree, out, base, messages, sums):
    tiles_dev = messages.shape[0] - 1
    messages[tiles_dev] = jnp.zeros(messages.shape[1:], BF16)
    per = (sums.shape[0] - tiles_dev) // Y
    body_rows = per * 8
    places = [FEAT_ORDER.index(f) * 16 for f in range(len(FEAT_ORDER))]
    dz = jnp.concatenate([dz[p : p + 16] for p in places], axis=0)
    sent = press(lax.dot_general(packed[:, : dz.shape[1]], dz, NT, preferred_element_type=F32))
    for peer in range(out.shape[0]):
        out[peer, body_rows:] = sent
    product = jnp.dot(packed[:, dz.shape[1] :], dz, preferred_element_type=F32)
    for t in range(tiles_dev):
        columns = slice(t * TILE, (t + 1) * TILE)
        messages[t] = (product[:16, columns] / degree[t, 0:1]).astype(BF16)
    sums[...] = jnp.zeros_like(sums)
    for k in range(tiles.shape[0]):
        block = messages[jnp.where(k < count[0], target[k], tiles_dev)]
        sums[source[k]] += jnp.dot(block, tiles[k], preferred_element_type=F32)
    for t in range(tiles_dev):
        columns = slice(t * TILE, (t + 1) * TILE)
        base[:, columns] = product[16:, columns] + sums[t]
    for y in range(Y):
        for q in range(per // 2):
            block = tiles_dev + y * per + 2 * q
            even, odd = exchange_halves(sums[block], sums[block + 1])
            out[NEAR_ORDER.index((y, 0)), q * 16 : (q + 1) * 16] = even
            out[NEAR_ORDER.index((y, 1)), q * 16 : (q + 1) * 16] = odd


def repack_kernel(got, out):
    pairs = out.shape[0]
    body_rows = pairs * 8
    total = jnp.zeros((got.shape[1] - body_rows, TILE), F32)
    for peer in range(got.shape[0]):
        total += release(got[peer, body_rows:])
    sent = press(total)
    for peer in range(pairs):
        out[peer, Y * 16 :] = sent
    for y in range(Y):
        for q in range(pairs // 2):
            a = got[NEAR_ORDER.index((y, 0)), q * 16 : (q + 1) * 16].astype(F32)
            b = got[NEAR_ORDER.index((y, 1)), q * 16 : (q + 1) * 16].astype(F32)
            low, high = exchange_halves(a, b)
            out[FAR_ORDER.index(2 * q), y * 16 : (y + 1) * 16] = low
            out[FAR_ORDER.index(2 * q + 1), y * 16 : (y + 1) * 16] = high


def scatter_kernel(got, hot, part, base, out, grad_w_self, grad_w_neigh):
    pairs = got.shape[0]
    tiles_dev = base.shape[1] // TILE
    total = jnp.zeros((tiles_dev * 16, TILE), F32)
    weight = jnp.zeros((got.shape[1] - Y * 16, TILE), F32)
    for y in range(Y):
        for p in range(0, pairs, 2):
            values = jnp.concatenate([got[FAR_ORDER.index(c), y * 16 : (y + 1) * 16] for c in (p, p + 1)], axis=1)
            k = (y * pairs + p) * TILE
            span = slice(k, k + 2 * TILE)
            where = part[:, span]
            spread = jnp.concatenate([jnp.where(where == t, values, jnp.zeros_like(values)) for t in range(tiles_dev)], axis=0)
            total += lax.dot_general(spread, hot[:, span], NT, preferred_element_type=F32)
    for peer in range(pairs):
        weight += release(got[peer, Y * 16 :])
    for t in range(tiles_dev):
        columns = slice(t * TILE, (t + 1) * TILE)
        out[:, columns] = base[:, columns] + total[t * 16 : (t + 1) * 16]
    grad_w_self[...] = weight[:16]
    grad_w_neigh[...] = weight[16:]


def call(kernel, outs, specs, *args, scratch=(), moved=0, limit=48):
    return pl.pallas_call(
        kernel,
        out_shape=outs,
        in_specs=specs,
        out_specs=jax.tree.map(lambda _: VMEM, outs),
        scratch_shapes=scratch,
        compiler_params=pltpu.CompilerParams(vmem_limit_bytes=limit * MIB),
        cost_estimate=pl.CostEstimate(flops=0, bytes_accessed=moved, transcendentals=0),
    )(*args)


def body(
    feats,
    aggregated,
    preact,
    grad_out,
    w_self,
    w_neigh,
    tile_values,
    tile_target,
    tile_source,
    tile_count,
    recv_rows,
    recv_count,
):
    width, nodes_dev = feats.shape
    ndom = lax.axis_size("dom")
    nfeat = lax.axis_size("feat")
    slots = recv_rows.shape[2]
    tiles_dev = nodes_dev // TILE
    halo_tiles = ndom * slots // TILE
    nz = ndom // Y
    pairs = nz // 2
    near = [[y * nz + 2 * p + odd for y, odd in NEAR_ORDER] for p in range(pairs)]
    far = [[y * nz + 2 * p + odd for p in FAR_ORDER] for y in range(Y) for odd in range(2)]
    shape = jax.ShapeDtypeStruct

    dz = call(
        gate_kernel,
        shape((nfeat, width, nodes_dev), BF16),
        [ANY] * 2,
        preact,
        grad_out,
        scratch=[pltpu.VMEM((width, nodes_dev), BF16)] * 2 + [pltpu.SemaphoreType.DMA((2,))],
        limit=60,
    )
    dz = lax.all_to_all(dz, "feat", 0, 0, tiled=True, axis_index_groups=[FEAT_ORDER]).reshape(nfeat * width, nodes_dev)
    packed = jnp.concatenate(
        [jnp.concatenate([feats, w_neigh], axis=1), jnp.concatenate([aggregated, w_self], axis=1)], axis=0
    )
    tiles, degree = call(
        prep_kernel,
        (shape(tile_values.shape, BF16), shape((tiles_dev, 8, TILE), F32)),
        [SMEM] * 2 + [ANY],
        tile_count,
        tile_target,
        tile_values,
        scratch=[pltpu.SemaphoreType.DMA((CHUNKS,))],
        moved=4000000,
        limit=51,
    )
    hot, part = call(
        route_kernel,
        (shape((TILE, ndom * slots), BF16), shape((16, ndom * slots), BF16)),
        [ANY] * 2,
        recv_rows,
        recv_count,
        scratch=[
            pltpu.VMEM((ndom, slots), jnp.int32),
            pltpu.SMEM((ndom,), jnp.int32),
            pltpu.SemaphoreType.DMA((2,)),
        ],
        moved=4000000,
    )

    out, base = call(
        tile_kernel,
        (shape((2 * Y, pairs * 8 + 2 * width, TILE), BF16), shape((width, nodes_dev), F32)),
        [SMEM] * 3 + [VMEM] * 4,
        tile_count,
        tile_target,
        tile_source,
        dz,
        packed,
        tiles,
        degree,
        scratch=[pltpu.VMEM((tiles_dev + 1, width, TILE), BF16), pltpu.VMEM((tiles_dev + halo_tiles, width, TILE), F32)],
    )
    got = lax.all_to_all(out, "dom", 0, 0, tiled=True, axis_index_groups=near)
    out = call(repack_kernel, shape((pairs, Y * 16 + 2 * width, TILE), BF16), [VMEM], got)
    got = lax.all_to_all(out, "dom", 0, 0, tiled=True, axis_index_groups=far)
    return call(
        scatter_kernel,
        (shape((width, nodes_dev), F32), shape((width, TILE), F32), shape((width, TILE), F32)),
        [VMEM] * 4,
        got,
        hot,
        part,
        base,
    )


def solution(mesh):
    return jax.shard_map(
        body,
        mesh=mesh,
        in_specs=(
            P("feat", "dom"),
            P("feat", "dom"),
            P("feat", "dom"),
            P("feat", "dom"),
            P("feat", None),
            P("feat", None),
            P("dom", None, None),
            P("dom"),
            P("dom"),
            P("dom"),
            P("dom", None, None),
            P("dom", None),
        ),
        out_specs=(P("feat", "dom"), P("feat", None), P("feat", None)),
        check_vma=False,
    )
```

```python
import jax
import jax.numpy as jnp
from jax import lax
from jax.experimental import pallas as pl
from jax.experimental.pallas import tpu as pltpu
from jax.sharding import PartitionSpec as P

TILE = 128
Y = 4
F32 = jnp.float32
BF16 = jnp.bfloat16
NT = (((1,), (1,)), ((), ()))
VMEM = pl.BlockSpec(memory_space=pltpu.VMEM)
ANY = pl.BlockSpec(memory_space=pl.ANY)
SMEM = pl.BlockSpec(memory_space=pltpu.SMEM)
MIB = 1024 * 1024
CHUNKS = 4


FEAT_ORDER = [3, 4, 5, 6, 7, 0, 1, 2]
NEAR_ORDER = [(2, 1), (2, 0), (3, 1), (3, 0), (0, 1), (0, 0), (1, 1), (1, 0)]
FAR_ORDER = [5, 3, 0, 4, 1, 7, 6, 2]


def split(x):
    high = x.astype(BF16)
    return high, (x - high.astype(F32)).astype(BF16)


def press(x):
    square = x * 2.0**13
    square = square * square
    return jnp.where(x < 0, -square * square, square * square).astype(BF16)


def release(x):
    x = x.astype(F32)
    root = jnp.sqrt(jnp.sqrt(jnp.abs(x))) * 2.0**-13
    return jnp.where(x < 0, -root, jnp.where(x > 0, root, 0.0))


def fetch(pairs, sems):
    copies = [pltpu.make_async_copy(src, dst, sems.at[i]) for i, (src, dst) in enumerate(pairs)]
    for copy in copies:
        copy.start()
    return copies


def gate_kernel(preact, grad_out, out, gate, grad, sems):
    for copy in fetch([(preact, gate), (grad_out, grad)], sems):
        copy.wait()
    dz = jnp.where(gate[...] > 0, grad[...], jnp.zeros_like(grad))
    for copy in range(out.shape[0]):
        out[copy] = dz


def prep_kernel(count, target, tiles_in, tiles, degree, sems):
    step = tiles.shape[0] // CHUNKS
    spans = [pl.ds(i * step, step) for i in range(CHUNKS)]
    copies = fetch([(tiles_in.at[span], tiles.at[span]) for span in spans], sems)
    degree[...] = jnp.zeros_like(degree)
    ones = jnp.ones((8, TILE), BF16)
    for i, copy in enumerate(copies):
        copy.wait()
        for k in range(i * step, (i + 1) * step):
            sums = lax.dot_general(ones, tiles[k], NT, preferred_element_type=F32)
            degree[target[k]] += jnp.where(k < count[0], sums, 0.0)
    degree[...] = jnp.maximum(degree[...], 1.0)


def route_kernel(recv_rows, recv_count, hot, part, rows, counts, sems):
    for copy in fetch([(recv_rows.at[0], rows), (recv_count.at[0], counts)], sems):
        copy.wait()
    slots = rows.shape[1]
    lane = lax.broadcasted_iota(jnp.int32, (1, slots), 1)
    sub = lax.broadcasted_iota(jnp.int32, (TILE, TILE), 0)
    for pair in range(rows.shape[0] // 2):
        halves = [jnp.where(lane < counts[s], rows[s : s + 1], -1) for s in (2 * pair, 2 * pair + 1)]
        row = jnp.concatenate(halves, axis=1)
        k = pair * TILE
        hot[:, k : k + TILE] = (jnp.broadcast_to(row & (TILE - 1), (TILE, TILE)) == sub).astype(F32).astype(BF16)
        part[:, k : k + TILE] = jnp.broadcast_to(row >> 7, (16, TILE)).astype(F32).astype(BF16)


def exchange_halves(a, b):
    first = lax.broadcasted_iota(jnp.int32, a.shape, 1) < TILE // 2
    low = jnp.where(first, a, pltpu.roll(b, TILE // 2, 1))
    return low.astype(BF16), jnp.where(first, pltpu.roll(a, TILE // 2, 1), b).astype(BF16)


def tile_kernel(count, target, source, dz, packed, tiles, degree, out, base, messages, sums):
    tiles_dev = messages.shape[0]
    per = (sums.shape[0] - tiles_dev) // Y
    body_rows = per * 8
    places = [FEAT_ORDER.index(f) * 16 for f in range(len(FEAT_ORDER))]
    dz = jnp.concatenate([dz[p : p + 16] for p in places], axis=0)
    sent = press(lax.dot_general(packed[:, : dz.shape[1]], dz, NT, preferred_element_type=F32))
    for peer in range(out.shape[0]):
        out[peer, body_rows:] = sent
    product = jnp.dot(packed[:, dz.shape[1] :], dz, preferred_element_type=F32)
    for t in range(tiles_dev):
        columns = slice(t * TILE, (t + 1) * TILE)
        messages[t] = (product[:16, columns] / degree[t, 0:1]).astype(BF16)
    sums[...] = jnp.zeros_like(sums)
    for k in range(tiles.shape[0]):
        block = messages[target[k]]
        block = jnp.where(k < count[0], block, jnp.zeros_like(block))
        sums[source[k]] += jnp.dot(block, tiles[k], preferred_element_type=F32)
    for t in range(tiles_dev):
        columns = slice(t * TILE, (t + 1) * TILE)
        base[:, columns] = product[16:, columns] + sums[t]
    for y in range(Y):
        for q in range(per // 2):
            block = tiles_dev + y * per + 2 * q
            even, odd = exchange_halves(sums[block], sums[block + 1])
            out[NEAR_ORDER.index((y, 0)), q * 16 : (q + 1) * 16] = even
            out[NEAR_ORDER.index((y, 1)), q * 16 : (q + 1) * 16] = odd


def repack_kernel(got, out):
    pairs = out.shape[0]
    body_rows = pairs * 8
    total = jnp.zeros((got.shape[1] - body_rows, TILE), F32)
    for peer in range(got.shape[0]):
        total += release(got[peer, body_rows:])
    sent = press(total)
    for peer in range(pairs):
        out[peer, Y * 16 :] = sent
    for y in range(Y):
        for q in range(pairs // 2):
            a = got[NEAR_ORDER.index((y, 0)), q * 16 : (q + 1) * 16].astype(F32)
            b = got[NEAR_ORDER.index((y, 1)), q * 16 : (q + 1) * 16].astype(F32)
            low, high = exchange_halves(a, b)
            out[FAR_ORDER.index(2 * q), y * 16 : (y + 1) * 16] = low
            out[FAR_ORDER.index(2 * q + 1), y * 16 : (y + 1) * 16] = high


def scatter_kernel(got, hot, part, base, out, grad_w_self, grad_w_neigh):
    pairs = got.shape[0]
    tiles_dev = base.shape[1] // TILE
    total = jnp.zeros((tiles_dev * 16, TILE), F32)
    weight = jnp.zeros((got.shape[1] - Y * 16, TILE), F32)
    for y in range(Y):
        for p in range(0, pairs, 4):
            values = jnp.concatenate([got[FAR_ORDER.index(c), y * 16 : (y + 1) * 16] for c in range(p, p + 4)], axis=1)
            k = (y * pairs + p) * TILE
            span = slice(k, k + 4 * TILE)
            where = part[:, span]
            spread = jnp.concatenate([jnp.where(where == t, values, jnp.zeros_like(values)) for t in range(tiles_dev)], axis=0)
            total += lax.dot_general(spread, hot[:, span], NT, preferred_element_type=F32)
    for peer in range(pairs):
        weight += release(got[peer, Y * 16 :])
    for t in range(tiles_dev):
        columns = slice(t * TILE, (t + 1) * TILE)
        out[:, columns] = base[:, columns] + total[t * 16 : (t + 1) * 16]
    grad_w_self[...] = weight[:16]
    grad_w_neigh[...] = weight[16:]


def call(kernel, outs, specs, *args, scratch=(), moved=0, limit=48):
    return pl.pallas_call(
        kernel,
        out_shape=outs,
        in_specs=specs,
        out_specs=jax.tree.map(lambda _: VMEM, outs),
        scratch_shapes=scratch,
        compiler_params=pltpu.CompilerParams(vmem_limit_bytes=limit * MIB),
        cost_estimate=pl.CostEstimate(flops=0, bytes_accessed=moved, transcendentals=0),
    )(*args)


def body(
    feats,
    aggregated,
    preact,
    grad_out,
    w_self,
    w_neigh,
    tile_values,
    tile_target,
    tile_source,
    tile_count,
    recv_rows,
    recv_count,
):
    width, nodes_dev = feats.shape
    ndom = lax.axis_size("dom")
    nfeat = lax.axis_size("feat")
    slots = recv_rows.shape[2]
    tiles_dev = nodes_dev // TILE
    halo_tiles = ndom * slots // TILE
    nz = ndom // Y
    pairs = nz // 2
    near = [[y * nz + 2 * p + odd for y, odd in NEAR_ORDER] for p in range(pairs)]
    far = [[y * nz + 2 * p + odd for p in FAR_ORDER] for y in range(Y) for odd in range(2)]
    shape = jax.ShapeDtypeStruct

    dz = call(
        gate_kernel,
        shape((nfeat, width, nodes_dev), BF16),
        [ANY] * 2,
        preact,
        grad_out,
        scratch=[pltpu.VMEM((width, nodes_dev), BF16)] * 2 + [pltpu.SemaphoreType.DMA((2,))],
        limit=60,
    )
    dz = lax.all_to_all(dz, "feat", 0, 0, tiled=True, axis_index_groups=[FEAT_ORDER]).reshape(nfeat * width, nodes_dev)
    packed = jnp.concatenate(
        [jnp.concatenate([feats, w_neigh], axis=1), jnp.concatenate([aggregated, w_self], axis=1)], axis=0
    )
    tiles, degree = call(
        prep_kernel,
        (shape(tile_values.shape, BF16), shape((tiles_dev, 8, TILE), F32)),
        [SMEM] * 2 + [ANY],
        tile_count,
        tile_target,
        tile_values,
        scratch=[pltpu.SemaphoreType.DMA((CHUNKS,))],
        moved=4000000,
        limit=51,
    )
    hot, part = call(
        route_kernel,
        (shape((TILE, ndom * slots), BF16), shape((16, ndom * slots), BF16)),
        [ANY] * 2,
        recv_rows,
        recv_count,
        scratch=[
            pltpu.VMEM((ndom, slots), jnp.int32),
            pltpu.SMEM((ndom,), jnp.int32),
            pltpu.SemaphoreType.DMA((2,)),
        ],
        moved=4000000,
    )

    out, base = call(
        tile_kernel,
        (shape((2 * Y, pairs * 8 + 2 * width, TILE), BF16), shape((width, nodes_dev), F32)),
        [SMEM] * 3 + [VMEM] * 4,
        tile_count,
        tile_target,
        tile_source,
        dz,
        packed,
        tiles,
        degree,
        scratch=[pltpu.VMEM((tiles_dev, width, TILE), BF16), pltpu.VMEM((tiles_dev + halo_tiles, width, TILE), F32)],
    )
    got = lax.all_to_all(out, "dom", 0, 0, tiled=True, axis_index_groups=near)
    out = call(repack_kernel, shape((pairs, Y * 16 + 2 * width, TILE), BF16), [VMEM], got)
    got = lax.all_to_all(out, "dom", 0, 0, tiled=True, axis_index_groups=far)
    return call(
        scatter_kernel,
        (shape((width, nodes_dev), F32), shape((width, TILE), F32), shape((width, TILE), F32)),
        [VMEM] * 4,
        got,
        hot,
        part,
        base,
    )


def solution(mesh):
    return jax.shard_map(
        body,
        mesh=mesh,
        in_specs=(
            P("feat", "dom"),
            P("feat", "dom"),
            P("feat", "dom"),
            P("feat", "dom"),
            P("feat", None),
            P("feat", None),
            P("dom", None, None),
            P("dom"),
            P("dom"),
            P("dom"),
            P("dom", None, None),
            P("dom", None),
        ),
        out_specs=(P("feat", "dom"), P("feat", None), P("feat", None)),
        check_vma=False,
    )
```
